512 devices in a mesh: ctx: 128 (over y_hi, z, x, core), tp: 4 (over y_lo).
Axes of the slice: x: 4, y: 8 (y_hi: 2, y_lo: 4; y = y_hi * 4 + y_lo), z: 8, core: 2. Of those that a mesh axis runs over, the one named last changes fastest.
Arguments:
- streams: bfloat16 [3, 4096, 16384], P(None, 'tp', 'ctx'), may hold values from -6 to 6
- conv_weight: float32 [3, 7, 4096], P(None, None, 'tp'), may hold values from -2 to 2
- rates: float32 [512, 16], P('tp'), may hold values from 1.2207031e-05 to 0.05
- residues: float32 [512, 16], P('tp'), may hold values from -4 to 4
- skip: float32 [4096], P('tp'), may hold values from -4 to 4
- out_weight: bfloat16 [4096, 4096], P('ctx', 'tp'), may hold values from -0.09375 to 0.09375
Outputs:
- result: bfloat16 [16384, 4096], P('ctx', 'tp')
The draws below stay inside these ranges and needn't reach their ends.
All inputs are finite; a program needn't handle non-finite values.
Results may differ from the reference program's by a relative error of at most 0.014.
Values may be sent and summed in bfloat16 or wider, within the bound.
A program may use at most 128 MiB of HBM per device.

```python
import math
import jax
import jax.numpy as jnp
from jax import lax

D = 4096
TAPS = 7
POLES = 16
FILTER_GROUPS = 512
TOKENS = 16384


def draw_rates(key, part):
    flag_key, slow_key, fast_key = jax.random.split(key, 3)
    slow_share = 0.5
    grid_shape = (FILTER_GROUPS, POLES)
    slow_rate = jnp.exp(jax.random.uniform(slow_key, grid_shape, jnp.float32, math.log(0.2 / TOKENS), math.log(2.0 / TOKENS)))
    fast_rate = jnp.exp(jax.random.uniform(fast_key, grid_shape, jnp.float32, math.log(0.02), math.log(0.05)))
    slow_pick = jax.random.uniform(flag_key, grid_shape, jnp.float32) < slow_share
    return jnp.where(slow_pick, slow_rate, fast_rate).astype(jnp.float32)


def level_of(rng, extent, cuts, smallest, top_value):
    level, own = 1.0, jax.random.fold_in(rng, 6)
    for axis_at, blocks in cuts:
        draws = jnp.exp(jax.random.uniform(jax.random.fold_in(own, axis_at), (blocks,), jnp.float32, smallest / len(cuts), top_value / len(cuts)))
        level = level * jnp.repeat(draws, extent[axis_at] // blocks).reshape([-1 if axis == axis_at else 1 for axis in range(len(extent))])
    return level


def gaussian(key, dims, deviation, bound, shards=(), kind=jnp.bfloat16):
    gain = level_of(key, dims, shards, -0.22, 0.18) if shards else 1.0
    drawn = jax.random.normal(key, dims, jnp.float32) * deviation * gain
    return jnp.minimum(jnp.maximum(drawn, -bound), bound).astype(kind)


def setup_inputs(seed: int = 0) -> dict:
    keys = jax.random.split(jax.random.key(seed), 7)
    streams = gaussian(keys[0], (3, D, TOKENS), 1.0, 6.0, ((1, 4), (2, 128)))
    conv_weight = gaussian(keys[1], (3, TAPS, D), TAPS ** -0.5, 2.0, ((2, 4),), jnp.float32)
    rates = draw_rates(jax.random.fold_in(keys[6], 71), 0)
    residues = gaussian(keys[3], (FILTER_GROUPS, POLES), 1.0, 4.0, ((0, 4),), jnp.float32)
    skip = gaussian(keys[4], (D,), 1.0, 4.0, ((0, 4),), jnp.float32)
    out_weight = gaussian(keys[5], (D, D), D ** -0.5, 0.09375, ((0, 128), (1, 4)))
    return {"streams": streams, "conv_weight": conv_weight, "rates": rates, "residues": residues, "skip": skip, "out_weight": out_weight}


def reference(streams, conv_weight, rates, residues, skip, out_weight):
    tap_count = conv_weight.shape[1]
    rim_width = tap_count - 1
    coefficient = residues * jnp.sqrt(2.0 * rates) / math.sqrt(POLES)
    group_width = D // FILTER_GROUPS
    block_chans = 256
    block_groups = block_chans // group_width

    def channel_block(block_index):
        first_chan = (block_index * block_chans).astype(jnp.int32)
        signal = lax.dynamic_slice_in_dim(streams, first_chan, block_chans, 1).astype(jnp.float32)
        taps_here = lax.dynamic_slice_in_dim(conv_weight, first_chan, block_chans, 2)
        padded = jnp.pad(signal, ((0, 0), (0, 0), (rim_width, 0)))
        filtered = jnp.zeros_like(signal)
        for shift_by in range(tap_count):
            filtered = filtered + taps_here[:, shift_by, :, None] * padded[:, :, rim_width - shift_by:rim_width - shift_by + TOKENS]
        queries = filtered[0]
        gated_in = (filtered[1] * filtered[2]).astype(jnp.bfloat16).astype(jnp.float32)
        first_group = (first_chan // group_width).astype(jnp.int32)
        coef_here = lax.dynamic_slice_in_dim(coefficient, first_group, block_groups, 0)
        rate_here = lax.dynamic_slice_in_dim(rates, first_group, block_groups, 0)
        position = jnp.arange(TOKENS, dtype=jnp.float32)
        kernel = jnp.einsum('gn,gnt->gt', coef_here, jnp.exp(-rate_here[:, :, None] * position), precision=lax.Precision.HIGHEST)
        kernel = jnp.repeat(kernel, group_width, axis=0)
        padded_len = 2 * TOKENS
        spectrum = jnp.fft.rfft(gated_in, n=padded_len, axis=1) * jnp.fft.rfft(kernel, n=padded_len, axis=1)
        longconv = jnp.fft.irfft(spectrum, n=padded_len, axis=1)[:, :TOKENS]
        skip_here = lax.dynamic_slice_in_dim(skip, first_chan, block_chans, 0)
        return (queries * (longconv + skip_here[:, None] * gated_in)).astype(jnp.bfloat16)
    mixed = lax.map(channel_block, jnp.arange(D // block_chans, dtype=jnp.int32))
    mixed = mixed.reshape(D, TOKENS)
    result = lax.dot_general(mixed, out_weight, (((0,), (0,)), ((), ())), preferred_element_type=jnp.float32)
    return result.astype(jnp.bfloat16)
```

```python
import functools
import math

import jax
import jax.numpy as jnp
from jax import lax
from jax.experimental import pallas as pl
from jax.experimental.pallas import tpu as pltpu
from jax.sharding import PartitionSpec as P

NZ, NX = 8, 4
LINE = NX * 2
LANES = 128
RIM = 8
HIGHEST = lax.Precision.HIGHEST


class Message:
    def __init__(self, sems, number, src, dst, land, to):
        send, recv = sems
        make = functools.partial(
            pltpu.make_async_remote_copy,
            send_sem=send.at[number],
            recv_sem=recv.at[number],
            device_id=to,
            device_id_type=pl.DeviceIdType.MESH,
        )
        self.out = make(src_ref=src, dst_ref=dst)
        self.into = make(src_ref=src, dst_ref=land)

    def start(self):
        self.out.start()

    def recv(self):
        self.into.wait_recv()

    def sent(self):
        self.out.wait_send()


def kernel(
    tap_count,
    streams,
    taps,
    rates,
    residues,
    skip,
    w_in,
    out,
    w,
    ext,
    rim,
    query,
    gated,
    conv,
    decay,
    coef,
    rate_chunks,
    ends,
    line_in,
    row_total,
    row_in,
    enter_out,
    enter_in,
    mixed,
    total,
    send_sems,
    recv_sems,
):
    poles = rates.shape[1]
    channels, tokens = streams.shape[1:]
    half = channels // 2
    rows = w_in.shape[0]
    ctx, tp = lax.axis_index("ctx"), lax.axis_index("tp")
    ctx_n, tp_n = lax.axis_size("ctx"), lax.axis_size("tp")
    core = ctx % 2
    x = (ctx // 2) % NX
    z = (ctx // LINE) % NZ
    y = ctx // (LINE * NZ)
    place = ctx % LINE
    row = ctx // LINE

    def at(y_=None, z_=None, x_=None, core_=None):
        y_ = y if y_ is None else y_
        z_ = z if z_ is None else z_
        x_ = x if x_ is None else x_
        core_ = core if core_ is None else core_
        return (((y_ * NZ + z_) * NX + x_) * 2 + core_, tp)

    def flip(value, bits):
        result = value * 0
        for bit in (1, 2, 4):
            digit = (value // bit) % 2
            result = result + bit * ((1 - digit) if bits & bit else digit)
        return result

    sems = (send_sems, recv_sems)
    count = [0]
    sent = []

    def message(src, dst, land, to):
        made = Message(sems, count[0], src, dst, land, to)
        count[0] += 1
        return made

    def start(made):
        made.start()
        sent.append(made)

    line_peers = [ctx - place + flip(place, m) for m in range(1, LINE)]
    row_peers = [
        ((y + dy) % 2 * NZ + flip(z, m)) * LINE + place
        for dy in range(2)
        for m in range(NZ)
        if (dy, m) != (0, 0)
    ]
    next_ctx, last_ctx = (ctx + 1) % ctx_n, (ctx + ctx_n - 1) % ctx_n
    peers = [(c, tp) for c in line_peers + row_peers + [next_ctx, last_ctx]]
    peers += [(ctx, (tp + 1) % tp_n), (ctx, (tp + tp_n - 1) % tp_n)]
    barrier = pltpu.get_barrier_semaphore()
    for peer in peers:
        pl.semaphore_signal(barrier, inc=1, device_id=peer, device_id_type=pl.DeviceIdType.MESH)
    pl.semaphore_wait(barrier, len(peers))

    groups = [(0, 1), (1, 2), (3, 2), (5, 2), (7, 1)]
    ups, downs = at(z_=(z + 1) % NZ), at(z_=(z + NZ - 1) % NZ)
    rights, lefts = at(x_=(x + 1) % NX), at(x_=(x + NX - 1) % NX)
    x_left, x_right = (x + NX - 1) % NX, (x + 1) % NX
    x_far = (x + 2) % NX
    sibling = at(core_=1 - core)
    top, bottom = pl.ds(0, rows // 2), pl.ds(rows // 2, rows // 2)

    across = message(
        w_in, w.at[y, 0, x, core], w.at[1 - y, 0, x, core], at(y_=1 - y)
    )
    start(across)
    w[y, 0, x, core] = w_in[...]

    def za(step):
        up_src, down_src = max(2 * step - 2, 0), max(2 * step - 3, 0)
        if step < 4:
            return (
                message(w.at[0, up_src, x, core], w.at[0, 2 * step, x, core], w.at[0, 2 * step, x, core], ups),
                message(w.at[0, down_src, x, core], w.at[0, 2 * step - 1, x, core], w.at[0, 2 * step - 1, x, core], downs),
            )
        return (
            message(w.at[0, 6, x, core, top], w.at[0, 7, x, core, top], w.at[0, 7, x, core, top], ups),
            message(w.at[0, 5, x, core, bottom], w.at[0, 7, x, core, bottom], w.at[0, 7, x, core, bottom], downs),
        )

    def xa(group):
        slots = pl.ds(*groups[group])
        mine = w.at[0, slots, x, core]
        return (
            message(mine, mine, w.at[0, slots, x_left, core], rights),
            message(mine, mine, w.at[0, slots, x_right, core], lefts),
        )

    def xa_far(group):
        slots = pl.ds(*groups[group])
        from_left = w.at[0, slots, x_left, core, top]
        from_right = w.at[0, slots, x_right, core, bottom]
        return (
            message(from_left, from_left, w.at[0, slots, x_far, core, top], rights),
            message(from_right, from_right, w.at[0, slots, x_far, core, bottom], lefts),
        )

    def xb():
        mine = w.at[1, 0, x, core]
        return (
            message(mine, mine, w.at[1, 0, x_left, core], rights),
            message(mine, mine, w.at[1, 0, x_right, core], lefts),
        )

    def xb_far():
        from_left = w.at[1, 0, x_left, core, top]
        from_right = w.at[1, 0, x_right, core, bottom]
        return (
            message(from_left, from_left, w.at[1, 0, x_far, core, top], rights),
            message(from_right, from_right, w.at[1, 0, x_far, core, bottom], lefts),
        )

    def zb(step):
        up_src, down_src = max(2 * step - 2, 0), max(2 * step - 3, 0)
        all_x = pl.ds(0, NX)
        if step < 4:
            return (
                message(w.at[1, up_src, all_x, core], w.at[1, 2 * step, all_x, core], w.at[1, 2 * step, all_x, core], ups),
                message(w.at[1, down_src, all_x, core], w.at[1, 2 * step - 1, all_x, core], w.at[1, 2 * step - 1, all_x, core], downs),
            )
        first, second = pl.ds(0, NX // 2), pl.ds(NX // 2, NX // 2)
        return (
            message(w.at[1, 6, first, core], w.at[1, 7, first, core], w.at[1, 7, first, core], ups),
            message(w.at[1, 5, second, core], w.at[1, 7, second, core], w.at[1, 7, second, core], downs),
        )

    def share(y_, group):
        slots = pl.ds(*groups[group])
        mine = w.at[y_, slots, pl.ds(0, NX), core]
        return (message(mine, mine, w.at[y_, slots, pl.ds(0, NX), 1 - core], sibling),)

    za_m = {s: za(s) for s in (1, 2, 3, 4)}
    xa_m = {g: xa(g) for g in range(5)}
    xaf_m = {g: xa_far(g) for g in range(5)}
    xb_m, xbf_m = xb(), xb_far()
    zb_m = {s: zb(s) for s in (1, 2, 3, 4)}
    share_m = {(y_, g): share(y_, g) for y_ in range(2) for g in range(5)}

    def start_all(pair):
        for made in pair:
            start(made)

    def recv_all(pair):
        for made in pair:
            made.recv()

    eye = (
        lax.broadcasted_iota(jnp.int32, (tokens, tokens), 0)
        == lax.broadcasted_iota(jnp.int32, (tokens, tokens), 1)
    ).astype(jnp.bfloat16)
    for s in range(3):
        ext[s, pl.ds(RIM, tokens), :] = lax.dot_general(
            eye, streams[s], (((1,), (1,)), ((), ())), preferred_element_type=jnp.float32
        )
    rim_m = message(ext.at[:, pl.ds(tokens, RIM), :], rim, rim, (next_ctx, tp))
    start(rim_m)

    across.recv()
    start_all(xb_m)
    start_all(za_m[1])
    start_all(xa_m[0])

    group_count = rates.shape[0]
    spread = (
        lax.broadcasted_iota(jnp.int32, (group_count, channels), 1) // (channels // group_count)
        == lax.broadcasted_iota(jnp.int32, (group_count, channels), 0)
    ).astype(jnp.float32)
    by_pole = (((0,), (0,)), ((), ()))
    rate = lax.dot_general(rates[...], spread, by_pole, precision=HIGHEST, preferred_element_type=jnp.float32)
    residue = lax.dot_general(residues[...], spread, by_pole, precision=HIGHEST, preferred_element_type=jnp.float32)
    decay[...] = jnp.exp(-rate)
    coef[...] = residue * jnp.sqrt(2.0 * rate) * (1.0 / math.sqrt(poles))
    for k in range(LINE):
        rate_chunks[k] = rate[:, k * LANES : (k + 1) * LANES]

    rim_m.recv()
    has_before = (ctx > 0).astype(jnp.float32)
    for s in range(3):
        ext[s, pl.ds(0, RIM), :] = rim[s] * has_before

    def short(k, carry):
        lanes = pl.ds(pl.multiple_of(k * LANES, LANES), LANES)

        def filtered(s):
            total_ = None
            for shift in range(tap_count):
                term = taps[s, pl.ds(shift, 1), lanes] * ext[s, pl.ds(RIM - shift, tokens), lanes]
                total_ = term if total_ is None else total_ + term
            return total_

        query[:, lanes] = filtered(0)
        gated[:, lanes] = (filtered(1) * filtered(2)).astype(jnp.bfloat16).astype(jnp.float32)
        return carry

    lax.fori_loop(0, channels // LANES, short, 0)

    unroll = 8
    for h in range(2):
        lanes = pl.ds(h * half, half)
        fall = decay[:, lanes]

        def step(t, state):
            for u in range(unroll):
                state = state * fall + gated[pl.ds(t * unroll + u, 1), lanes]
            return state

        state = lax.fori_loop(0, tokens // unroll, step, jnp.zeros((poles, half), jnp.float32))
        for k in range(half // LANES):
            ends[h * (half // LANES) + k] = state[:, k * LANES : (k + 1) * LANES]

    round1 = []
    for m in range(1, LINE):
        to = flip(place, m)
        round1.append(message(ends.at[to], line_in.at[place], line_in.at[to], (ctx - place + to, tp)))
    start_all(round1)
    line_in[place] = ends[place]

    recv_all(xb_m)
    start_all(xbf_m)
    recv_all(za_m[1])
    start_all(za_m[2])
    start_all(xa_m[1])

    recv_all(round1)
    my_rate = rate_chunks[place]
    block_fall = jnp.exp(my_rate * (-float(tokens)))
    row_fall = jnp.exp(my_rate * (-float(tokens * LINE)))
    state = line_in[0]
    for p in range(1, LINE):
        state = state * block_fall + line_in[p]
    row_total[...] = state
    row_in[row] = state

    round2 = []
    for dy in range(2):
        for m in range(NZ):
            if (dy, m) == (0, 0):
                continue
            other = (y + dy) % 2 * NZ + flip(z, m)
            round2.append(message(row_total, row_in.at[row], row_in.at[other], (other * LINE + place, tp)))
    start_all(round2)

    recv_all(xa_m[0])
    start_all(xaf_m[0])
    recv_all(xbf_m)
    start_all(zb_m[1])
    recv_all(za_m[2])
    start_all(za_m[3])
    start_all(xa_m[2])

    recv_all(round2)
    state = jnp.zeros((poles, LANES), jnp.float32)
    for r in range(2 * NZ - 1):
        state = jnp.where(r < row, state * row_fall + row_in[r], state)
    for p in range(LINE):
        enter_out[p] = state
        if p < LINE - 1:
            state = state * block_fall + line_in[p]

    round3 = []
    for m in range(1, LINE):
        to = flip(place, m)
        round3.append(message(enter_out.at[to], enter_in.at[place], enter_in.at[to], (ctx - place + to, tp)))
    start_all(round3)
    enter_in[place] = enter_out[place]

    recv_all(xa_m[1])
    start_all(xaf_m[1])
    recv_all(za_m[3])
    start_all(za_m[4])
    start_all(xa_m[3])

    recv_all(round3)

    right_m, left_m = {}, {}
    right_to, left_to = (ctx, (tp + 1) % tp_n), (ctx, (tp + tp_n - 1) % tp_n)
    for h in range(2):
        for d in range(3):
            behind, ahead = (tp + tp_n - d) % tp_n, (tp + d) % tp_n
            right_m[h, d] = message(
                mixed.at[h, behind], mixed.at[h, behind], mixed.at[h, (tp + tp_n - 1 - d) % tp_n], right_to
            )
            left_m[h, d] = message(
                mixed.at[h, ahead], mixed.at[h, ahead], mixed.at[h, (tp + 1 + d) % tp_n], left_to
            )

    def line_send(h, d):
        @pl.when((tp < tp_n - 1) & (tp >= d))
        def _():
            right_m[h, d].start()

        @pl.when((tp > 0) & (tp + d < tp_n))
        def _():
            left_m[h, d].start()

    def line_sent(h, d):
        @pl.when((tp < tp_n - 1) & (tp >= d))
        def _():
            right_m[h, d].sent()

        @pl.when((tp > 0) & (tp + d < tp_n))
        def _():
            left_m[h, d].sent()

    def line_recv(h, d):
        @pl.when(tp >= d + 1)
        def _():
            right_m[h, d].recv()

        @pl.when(tp + d + 1 < tp_n)
        def _():
            left_m[h, d].recv()

    for h in range(2):
        lanes = pl.ds(h * half, half)
        fall, gain = decay[:, lanes], coef[:, lanes]
        first = h * (half // LANES)
        enter = jnp.concatenate([enter_in[first + k] for k in range(half // LANES)], axis=1)

        def step(t, state):
            for u in range(unroll):
                at_t = pl.ds(t * unroll + u, 1)
                state = state * fall + gated[at_t, lanes]
                conv[at_t, lanes] = jnp.sum(state * gain, axis=0, keepdims=True)
            return state

        lax.fori_loop(0, tokens // unroll, step, enter)
        mixed[h, tp] = (
            query[:, lanes] * (conv[:, lanes] + skip[:, lanes] * gated[:, lanes])
        ).astype(jnp.bfloat16)
        line_send(h, 0)

    recv_all(zb_m[1])
    start_all(zb_m[2])
    start_all(share_m[1, 0])
    start_all(share_m[1, 1])
    recv_all(xa_m[2])
    start_all(xaf_m[2])
    recv_all(za_m[4])
    start_all(xa_m[4])
    for h in range(2):
        line_recv(h, 0)
        line_send(h, 1)
    recv_all(zb_m[2])
    start_all(zb_m[3])
    start_all(share_m[1, 2])
    recv_all(xa_m[3])
    start_all(xaf_m[3])
    recv_all(xa_m[4])
    start_all(xaf_m[4])
    for h in range(2):
        line_recv(h, 1)
        line_send(h, 2)
    recv_all(zb_m[3])
    start_all(zb_m[4])
    start_all(share_m[1, 3])
    for g in range(5):
        recv_all(xaf_m[g])
        start_all(share_m[0, g])
    recv_all(zb_m[4])
    start_all(share_m[1, 4])
    for h in range(2):
        line_recv(h, 2)
    for key in share_m:
        recv_all(share_m[key])

    total[...] = jnp.zeros_like(total)

    def project(k, carry):
        y_, z_ = k // NZ, k % NZ
        behind = (z_ + NZ - z) % NZ
        slot = jnp.where(behind <= 4, jnp.maximum(2 * behind - 1, 0), 2 * (NZ - behind))
        block, rest = k // 4, k % 4
        weights = w[y_, slot].reshape(LINE * rows, w.shape[-1])
        part = pl.ds(pl.multiple_of((rest % 2) * (LINE * rows), LINE * rows), LINE * rows)
        total[...] += jnp.dot(
            mixed[rest // 2, block, :, part], weights, preferred_element_type=jnp.float32
        )
        return carry

    lax.fori_loop(0, 2 * NZ, project, 0)
    out[...] = total[...].astype(jnp.bfloat16)

    for made in sent:
        made.sent()
    for h in range(2):
        for d in range(3):
            line_sent(h, d)


def local(streams, conv_weight, rates, residues, skip, out_weight):
    channels, tokens = streams.shape[1:]
    poles = rates.shape[1]
    rows, features = out_weight.shape
    vmem = pl.BlockSpec(memory_space=pltpu.VMEM)
    f32, bf16 = jnp.float32, jnp.bfloat16
    messages = 1 + 8 + 20 + 4 + 8 + 10 + 1 + 7 + 15 + 7 + 12
    return pl.pallas_call(
        functools.partial(kernel, conv_weight.shape[1]),
        out_shape=jax.ShapeDtypeStruct((tokens, features), bf16),
        in_specs=[vmem] * 6,
        out_specs=vmem,
        scratch_shapes=[
            pltpu.VMEM((2, NZ, NX, 2, rows, features), bf16),
            pltpu.VMEM((3, RIM + tokens, channels), f32),
            pltpu.VMEM((3, RIM, channels), f32),
            pltpu.VMEM((tokens, channels), f32),
            pltpu.VMEM((tokens, channels), f32),
            pltpu.VMEM((tokens, channels), f32),
            pltpu.VMEM((poles, channels), f32),
            pltpu.VMEM((poles, channels), f32),
            pltpu.VMEM((LINE, poles, LANES), f32),
            pltpu.VMEM((LINE, poles, LANES), f32),
            pltpu.VMEM((LINE, poles, LANES), f32),
            pltpu.VMEM((poles, LANES), f32),
            pltpu.VMEM((2 * NZ, poles, LANES), f32),
            pltpu.VMEM((LINE, poles, LANES), f32),
            pltpu.VMEM((LINE, poles, LANES), f32),
            pltpu.VMEM((2, 4, tokens, channels // 2), bf16),
            pltpu.VMEM((tokens, features), f32),
            pltpu.SemaphoreType.DMA((messages,)),
            pltpu.SemaphoreType.DMA((messages,)),
        ],
        compiler_params=pltpu.CompilerParams(
            collective_id=0, has_side_effects=True, vmem_limit_bytes=48 * 1024 * 1024
        ),
        cost_estimate=pl.CostEstimate(
            flops=2 * tokens * 4 * channels * features, bytes_accessed=12 << 20, transcendentals=1 << 15
        ),
    )(streams, conv_weight, rates, residues, skip.reshape(1, channels), out_weight)


def solution(mesh):
    return jax.shard_map(
        local,
        mesh=mesh,
        in_specs=(
            P(None, "tp", "ctx"),
            P(None, None, "tp"),
            P("tp", None),
            P("tp", None),
            P("tp"),
            P("ctx", "tp"),
        ),
        out_specs=P("ctx", "tp"),
        check_vma=False,
    )
```

```python
import functools
import math

import jax
import jax.numpy as jnp
from jax import lax
from jax.experimental import pallas as pl
from jax.experimental.pallas import tpu as pltpu
from jax.sharding import PartitionSpec as P

NZ, NX = 8, 4
LINE = NX * 2
LANES = 128
RIM = 8
HIGHEST = lax.Precision.HIGHEST


class Message:
    def __init__(self, sems, number, src, dst, land, to):
        send, recv = sems
        make = functools.partial(
            pltpu.make_async_remote_copy,
            send_sem=send.at[number],
            recv_sem=recv.at[number],
            device_id=to,
            device_id_type=pl.DeviceIdType.MESH,
        )
        self.out = make(src_ref=src, dst_ref=dst)
        self.into = make(src_ref=src, dst_ref=land)

    def start(self):
        self.out.start()

    def recv(self):
        self.into.wait_recv()

    def sent(self):
        self.out.wait_send()


def kernel(
    tap_count,
    streams_hbm,
    taps_hbm,
    rates_hbm,
    residues_hbm,
    skip_hbm,
    w_hbm,
    out,
    w,
    streams,
    taps,
    rates,
    residues,
    skip,
    ext,
    query,
    gated,
    conv,
    decay,
    coef,
    rate_chunks,
    ends,
    line_in,
    row_total,
    row_in,
    part_total,
    part_in,
    enter_out,
    enter_in,
    mixed,
    total,
    load_sems,
    send_sems,
    recv_sems,
):
    poles = rates.shape[0]
    channels, tokens = streams.shape[1:]
    half = channels // 2
    rows = w_hbm.shape[0]
    ctx, tp = lax.axis_index("ctx"), lax.axis_index("tp")
    ctx_n, tp_n = lax.axis_size("ctx"), lax.axis_size("tp")
    core = ctx % 2
    x = (ctx // 2) % NX
    z = (ctx // LINE) % NZ
    y = ctx // (LINE * NZ)
    place = ctx % LINE

    def at(y_=None, z_=None, x_=None, core_=None):
        y_ = y if y_ is None else y_
        z_ = z if z_ is None else z_
        x_ = x if x_ is None else x_
        core_ = core if core_ is None else core_
        return (((y_ * NZ + z_) * NX + x_) * 2 + core_, tp)

    def flip(value, bits):
        result = value * 0
        for bit in (1, 2, 4):
            digit = (value // bit) % 2
            result = result + bit * ((1 - digit) if bits & bit else digit)
        return result

    sems = (send_sems, recv_sems)
    count = [0]
    sent = []

    def message(src, dst, land, to):
        made = Message(sems, count[0], src, dst, land, to)
        count[0] += 1
        return made

    def start_all(pair):
        for made in pair:
            made.start()
            sent.append(made)

    def recv_all(pair):
        for made in pair:
            made.recv()

    barrier = pltpu.get_barrier_semaphore()

    def greet(peer):
        pl.semaphore_signal(barrier, inc=1, device_id=peer, device_id_type=pl.DeviceIdType.MESH)

    always = [at(y_=1 - y)]
    always += [(ctx - place + flip(place, m), tp) for m in range(1, LINE)]
    always += [at(z_=flip(z, m)) for m in range(1, NZ)]
    sometimes = [
        (ctx < ctx_n - 1, (ctx + 1, tp)),
        (ctx > 0, (ctx - 1, tp)),
        (tp < tp_n - 1, (ctx, tp + 1)),
        (tp > 0, (ctx, tp - 1)),
    ]
    greetings = len(always)
    for peer in always:
        greet(peer)
    for there, peer in sometimes:
        pl.when(there)(functools.partial(greet, peer))
        greetings = greetings + there.astype(jnp.int32)

    loads = [
        pltpu.make_async_copy(src, dst, load_sems.at[n])
        for n, (src, dst) in enumerate(
            [
                (w_hbm, w.at[y, 0, x, core]),
                (streams_hbm, streams),
                (rates_hbm, rates),
                (residues_hbm, residues),
                (taps_hbm, taps),
                (skip_hbm, skip),
            ]
        )
    ]
    for load in loads:
        load.start()

    groups = [(0, 1), (1, 2), (3, 2), (5, 2), (7, 1)]
    ups, downs = at(z_=(z + 1) % NZ), at(z_=(z + NZ - 1) % NZ)
    rights, lefts = at(x_=(x + 1) % NX), at(x_=(x + NX - 1) % NX)
    x_left, x_right = (x + NX - 1) % NX, (x + 1) % NX
    x_far = (x + 2) % NX
    sibling = at(core_=1 - core)
    top, bottom = pl.ds(0, rows // 2), pl.ds(rows // 2, rows // 2)
    own, other = y, 1 - y

    across = (message(w.at[own, 0, x, core], w.at[own, 0, x, core], w.at[other, 0, x, core], at(y_=other)),)

    def za(step):
        up_src, down_src = max(2 * step - 2, 0), max(2 * step - 3, 0)
        if step < 4:
            up_dst, down_dst = w.at[other, 2 * step, x, core], w.at[other, 2 * step - 1, x, core]
            return (
                message(w.at[other, up_src, x, core], up_dst, up_dst, ups),
                message(w.at[other, down_src, x, core], down_dst, down_dst, downs),
            )
        up_dst, down_dst = w.at[other, 7, x, core, top], w.at[other, 7, x, core, bottom]
        return (
            message(w.at[other, 6, x, core, top], up_dst, up_dst, ups),
            message(w.at[other, 5, x, core, bottom], down_dst, down_dst, downs),
        )

    def xa(y_, group):
        slots = pl.ds(*groups[group])
        mine = w.at[y_, slots, x, core]
        return (
            message(mine, mine, w.at[y_, slots, x_left, core], rights),
            message(mine, mine, w.at[y_, slots, x_right, core], lefts),
        )

    def xa_far(y_, group):
        slots = pl.ds(*groups[group])
        from_left = w.at[y_, slots, x_left, core, top]
        from_right = w.at[y_, slots, x_right, core, bottom]
        return (
            message(from_left, from_left, w.at[y_, slots, x_far, core, top], rights),
            message(from_right, from_right, w.at[y_, slots, x_far, core, bottom], lefts),
        )

    def zb(step):
        up_src, down_src = max(2 * step - 2, 0), max(2 * step - 3, 0)
        if step < 4:
            every = pl.ds(0, NX)
            up_dst, down_dst = w.at[own, 2 * step, every, core], w.at[own, 2 * step - 1, every, core]
            return (
                message(w.at[own, up_src, every, core], up_dst, up_dst, ups),
                message(w.at[own, down_src, every, core], down_dst, down_dst, downs),
            )
        first, second = pl.ds(0, NX // 2), pl.ds(NX // 2, NX // 2)
        up_dst, down_dst = w.at[own, 7, first, core], w.at[own, 7, second, core]
        return (
            message(w.at[own, 6, first, core], up_dst, up_dst, ups),
            message(w.at[own, 5, second, core], down_dst, down_dst, downs),
        )

    def share(y_, group):
        slots = pl.ds(*groups[group])
        mine = w.at[y_, slots, pl.ds(0, NX), core]
        return (message(mine, mine, w.at[y_, slots, pl.ds(0, NX), 1 - core], sibling),)

    za_m = {s: za(s) for s in (1, 2, 3, 4)}
    xa_m = {g: xa(other, g) for g in range(5)}
    xaf_m = {g: xa_far(other, g) for g in range(5)}
    xb_m, xbf_m = xa(own, 0), xa_far(own, 0)
    zb_m = {s: zb(s) for s in (1, 2, 3, 4)}
    own_share = {g: share(own, g) for g in range(5)}
    other_share = {g: share(other, g) for g in range(5)}

    rim_m = message(ext.at[:, pl.ds(tokens, RIM), :], ext.at[:, pl.ds(0, RIM), :], ext.at[:, pl.ds(0, RIM), :], (ctx + 1, tp))
    eye = (
        lax.broadcasted_iota(jnp.int32, (tokens, tokens), 0)
        == lax.broadcasted_iota(jnp.int32, (tokens, tokens), 1)
    ).astype(jnp.bfloat16)
    loads[0].wait()
    loads[1].wait()
    for s in range(3):
        ext[s, pl.ds(RIM, tokens), :] = lax.dot_general(
            eye, streams[s], (((1,), (1,)), ((), ())), preferred_element_type=jnp.float32
        )
    pl.semaphore_wait(barrier, greetings)

    pl.when(ctx < ctx_n - 1)(rim_m.start)
    start_all(across)
    start_all(xb_m)

    for load in loads[2:]:
        load.wait()
    group_count = rates.shape[1]
    spread = (
        lax.broadcasted_iota(jnp.int32, (group_count, channels), 1) // (channels // group_count)
        == lax.broadcasted_iota(jnp.int32, (group_count, channels), 0)
    ).astype(jnp.float32)
    plain = (((1,), (0,)), ((), ()))
    rate = lax.dot_general(rates[...], spread, plain, precision=HIGHEST, preferred_element_type=jnp.float32)
    residue = lax.dot_general(residues[...], spread, plain, precision=HIGHEST, preferred_element_type=jnp.float32)
    decay[...] = jnp.exp(-rate)
    coef[...] = residue * jnp.sqrt(2.0 * rate) * (1.0 / math.sqrt(poles))
    for k in range(LINE):
        rate_chunks[k] = rate[:, k * LANES : (k + 1) * LANES]

    def short_rows(first, length):
        def short(k, carry):
            lanes = pl.ds(pl.multiple_of(k * LANES, LANES), LANES)

            def filtered(s):
                total_ = None
                for shift in range(tap_count):
                    term = taps[s, pl.ds(shift, 1), lanes] * ext[s, pl.ds(RIM + first - shift, length), lanes]
                    total_ = term if total_ is None else total_ + term
                return total_

            at_rows = pl.ds(first, length)
            query[at_rows, lanes] = filtered(0)
            gated[at_rows, lanes] = (filtered(1) * filtered(2)).astype(jnp.bfloat16).astype(jnp.float32)
            return carry

        lax.fori_loop(0, channels // LANES, short, 0)

    unroll = 8

    def run_states(first, length, lanes, state):
        fall = decay[:, lanes]

        def step(t, state):
            for u in range(unroll):
                state = state * fall + gated[pl.ds(first + t * unroll + u, 1), lanes]
            return state

        return lax.fori_loop(0, length // unroll, step, state)

    short_rows(RIM, tokens - RIM)
    halves = [pl.ds(h * half, half) for h in range(2)]
    zeros = jnp.zeros((poles, half), jnp.float32)
    for h in range(2):
        state = run_states(RIM, tokens - RIM, halves[h], zeros)
        for k in range(half // LANES):
            ends[h * (half // LANES) + k] = state[:, k * LANES : (k + 1) * LANES]

    @pl.when(ctx > 0)
    def _():
        rim_m.recv()

    @pl.when(ctx == 0)
    def _():
        for s in range(3):
            ext[s, pl.ds(0, RIM), :] = jnp.zeros((RIM, channels), jnp.float32)

    short_rows(0, RIM)
    for h in range(2):
        state = run_states(0, RIM, halves[h], zeros)
        for k in range(half // LANES):
            n = h * (half // LANES) + k
            ends[n] += state[:, k * LANES : (k + 1) * LANES] * jnp.exp(rate_chunks[n] * (-float(tokens - RIM)))

    round1 = []
    for m in range(1, LINE):
        to = flip(place, m)
        round1.append(message(ends.at[to], line_in.at[place], line_in.at[to], (ctx - place + to, tp)))
    start_all(round1)
    line_in[place] = ends[place]

    recv_all(xb_m)
    start_all(xbf_m)

    recv_all(round1)
    my_rate = rate_chunks[place]
    block_fall = jnp.exp(my_rate * (-float(tokens)))
    row_fall = jnp.exp(my_rate * (-float(tokens * LINE)))
    state = line_in[0]
    for p in range(1, LINE):
        state = state * block_fall + line_in[p]
    row_total[...] = state
    row_in[z] = state

    round2 = []
    for m in range(1, NZ):
        to = flip(z, m)
        round2.append(message(row_total, row_in.at[z], row_in.at[to], at(z_=to)))
    start_all(round2)

    recv_all(xbf_m)
    start_all(zb_m[1])
    recv_all(across)
    start_all(za_m[1])
    start_all(xa_m[0])

    recv_all(round2)
    onward = message(part_total, part_in, part_in, at(y_=1 - y))

    @pl.when(y == 0)
    def _():
        state = row_in[0]
        for r in range(1, NZ):
            state = state * row_fall + row_in[r]
        part_total[...] = state
        onward.start()
        part_in[...] = jnp.zeros_like(part_in)

    recv_all(za_m[1])
    start_all(za_m[2])
    start_all(xa_m[1])
    recv_all(xa_m[0])
    start_all(xaf_m[0])

    @pl.when(y == 1)
    def _():
        onward.recv()

    state = part_in[...]
    for r in range(NZ - 1):
        state = jnp.where(r < z, state * row_fall + row_in[r], state)
    for p in range(LINE):
        enter_out[p] = state
        if p < LINE - 1:
            state = state * block_fall + line_in[p]

    round3 = []
    for m in range(1, LINE):
        to = flip(place, m)
        round3.append(message(enter_out.at[to], enter_in.at[place], enter_in.at[to], (ctx - place + to, tp)))
    start_all(round3)
    enter_in[place] = enter_out[place]

    recv_all(za_m[2])
    start_all(za_m[3])
    start_all(xa_m[2])
    recv_all(xa_m[1])
    start_all(xaf_m[1])

    recv_all(round3)

    right_m, left_m = {}, {}
    for h in range(2):
        for d in range(3):
            behind, ahead = (tp + tp_n - d) % tp_n, (tp + d) % tp_n
            right_m[h, d] = message(
                mixed.at[h, behind], mixed.at[h, behind], mixed.at[h, (tp + tp_n - 1 - d) % tp_n], (ctx, (tp + 1) % tp_n)
            )
            left_m[h, d] = message(
                mixed.at[h, ahead], mixed.at[h, ahead], mixed.at[h, (tp + 1 + d) % tp_n], (ctx, (tp + tp_n - 1) % tp_n)
            )

    def line_send(h, d):
        pl.when((tp < tp_n - 1) & (tp >= d))(right_m[h, d].start)
        pl.when((tp > 0) & (tp + d < tp_n))(left_m[h, d].start)

    def line_sent(h, d):
        pl.when((tp < tp_n - 1) & (tp >= d))(right_m[h, d].sent)
        pl.when((tp > 0) & (tp + d < tp_n))(left_m[h, d].sent)

    def line_recv(h, d):
        pl.when(tp >= d + 1)(right_m[h, d].recv)
        pl.when(tp + d + 1 < tp_n)(left_m[h, d].recv)

    for h in range(2):
        lanes = halves[h]
        fall, gain = decay[:, lanes], coef[:, lanes]
        first = h * (half // LANES)
        enter = jnp.concatenate([enter_in[first + k] for k in range(half // LANES)], axis=1)

        def step(t, state):
            for u in range(unroll):
                at_t = pl.ds(t * unroll + u, 1)
                state = state * fall + gated[at_t, lanes]
                conv[at_t, lanes] = jnp.sum(state * gain, axis=0, keepdims=True)
            return state

        lax.fori_loop(0, tokens // unroll, step, enter)
        mixed[h, tp] = (
            query[:, lanes] * (conv[:, lanes] + skip[:, lanes] * gated[:, lanes])
        ).astype(jnp.bfloat16)
        line_send(h, 0)

    recv_all(zb_m[1])
    start_all(zb_m[2])
    start_all(own_share[0])
    start_all(own_share[1])
    recv_all(za_m[3])
    start_all(za_m[4])
    start_all(xa_m[3])
    recv_all(xa_m[2])
    start_all(xaf_m[2])
    line_recv(0, 0)
    line_send(0, 1)
    recv_all(za_m[4])
    start_all(xa_m[4])
    line_recv(1, 0)
    line_send(1, 1)
    recv_all(zb_m[2])
    start_all(zb_m[3])
    start_all(own_share[2])
    recv_all(xa_m[3])
    start_all(xaf_m[3])
    line_recv(0, 1)
    line_send(0, 2)
    recv_all(xa_m[4])
    start_all(xaf_m[4])
    line_recv(1, 1)
    line_send(1, 2)
    recv_all(zb_m[3])
    start_all(zb_m[4])
    start_all(own_share[3])
    for g in range(5):
        recv_all(xaf_m[g])
        start_all(other_share[g])
    recv_all(zb_m[4])
    start_all(own_share[4])
    for g in range(5):
        recv_all(own_share[g])
        recv_all(other_share[g])

    deep = LINE * rows

    def project(h, block):
        def step(k, carry):
            place_ = block * 4 + h * 2 + k
            y_, z_ = place_ // NZ, place_ % NZ
            behind = (z_ + NZ - z) % NZ
            slot = jnp.where(behind <= 4, jnp.maximum(2 * behind - 1, 0), 2 * (NZ - behind))
            weights = w[y_, slot].reshape(deep, w.shape[-1])
            part = pl.ds(pl.multiple_of(k * deep, deep), deep)
            total[...] += jnp.dot(mixed[h, block, :, part], weights, preferred_element_type=jnp.float32)
            return carry

        lax.fori_loop(0, 2, step, 0)

    total[...] = jnp.zeros_like(total)
    for h in range(2):
        project(h, tp)
    for d in range(3):
        for h in range(2):
            if d == 2:
                line_recv(h, d)

            @pl.when(tp >= d + 1)
            def _():
                project(h, tp - 1 - d)

            @pl.when(tp + d + 1 < tp_n)
            def _():
                project(h, tp + 1 + d)

    out[...] = total[...].astype(jnp.bfloat16)

    for made in sent:
        made.sent()
    pl.when(ctx < ctx_n - 1)(rim_m.sent)
    pl.when(y == 0)(onward.sent)
    for h in range(2):
        for d in range(3):
            line_sent(h, d)


def local(streams, conv_weight, rates, residues, skip, out_weight):
    channels, tokens = streams.shape[1:]
    groups, poles = rates.shape
    rows, features = out_weight.shape
    anywhere = pl.BlockSpec(memory_space=pl.ANY)
    f32, bf16 = jnp.float32, jnp.bfloat16
    messages = 1 + 8 + 20 + 4 + 8 + 10 + 1 + 7 + 7 + 1 + 7 + 12
    return pl.pallas_call(
        functools.partial(kernel, conv_weight.shape[1]),
        out_shape=jax.ShapeDtypeStruct((tokens, features), bf16),
        in_specs=[anywhere] * 6,
        out_specs=pl.BlockSpec(memory_space=pltpu.VMEM),
        scratch_shapes=[
            pltpu.VMEM((2, NZ, NX, 2, rows, features), bf16),
            pltpu.VMEM(streams.shape, bf16),
            pltpu.VMEM(conv_weight.shape, f32),
            pltpu.VMEM((poles, groups), f32),
            pltpu.VMEM((poles, groups), f32),
            pltpu.VMEM((1, channels), f32),
            pltpu.VMEM((3, RIM + tokens, channels), f32),
            pltpu.VMEM((tokens, channels), f32),
            pltpu.VMEM((tokens, channels), f32),
            pltpu.VMEM((tokens, channels), f32),
            pltpu.VMEM((poles, channels), f32),
            pltpu.VMEM((poles, channels), f32),
            pltpu.VMEM((LINE, poles, LANES), f32),
            pltpu.VMEM((LINE, poles, LANES), f32),
            pltpu.VMEM((LINE, poles, LANES), f32),
            pltpu.VMEM((poles, LANES), f32),
            pltpu.VMEM((NZ, poles, LANES), f32),
            pltpu.VMEM((poles, LANES), f32),
            pltpu.VMEM((poles, LANES), f32),
            pltpu.VMEM((LINE, poles, LANES), f32),
            pltpu.VMEM((LINE, poles, LANES), f32),
            pltpu.VMEM((2, 4, tokens, channels // 2), bf16),
            pltpu.VMEM((tokens, features), f32),
            pltpu.SemaphoreType.DMA((6,)),
            pltpu.SemaphoreType.DMA((messages,)),
            pltpu.SemaphoreType.DMA((messages,)),
        ],
        compiler_params=pltpu.CompilerParams(
            collective_id=0, has_side_effects=True, vmem_limit_bytes=60 * 1024 * 1024
        ),
        cost_estimate=pl.CostEstimate(
            flops=2 * tokens * 4 * channels * features, bytes_accessed=12 << 20, transcendentals=1 << 15
        ),
    )(streams, conv_weight, rates.T, residues.T, skip.reshape(1, channels), out_weight)


def solution(mesh):
    return jax.shard_map(
        local,
        mesh=mesh,
        in_specs=(
            P(None, "tp", "ctx"),
            P(None, None, "tp"),
            P("tp", None),
            P("tp", None),
            P("tp"),
            P("ctx", "tp"),
        ),
        out_specs=P("ctx", "tp"),
        check_vma=False,
    )
```

```python
import functools
import math

import jax
import jax.numpy as jnp
from jax import lax
from jax.experimental import pallas as pl
from jax.experimental.pallas import tpu as pltpu
from jax.sharding import PartitionSpec as P

NZ, NX = 8, 4
LINE = NX * 2
LANES = 128
RIM = 8
HIGHEST = lax.Precision.HIGHEST


class Message:
    def __init__(self, sems, number, src, dst, land, to):
        send, recv = sems
        make = functools.partial(
            pltpu.make_async_remote_copy,
            send_sem=send.at[number],
            recv_sem=recv.at[number],
            device_id=to,
            device_id_type=pl.DeviceIdType.MESH,
        )
        self.out = make(src_ref=src, dst_ref=dst)
        self.into = make(src_ref=src, dst_ref=land)

    def start(self):
        self.out.start()

    def recv(self):
        self.into.wait_recv()

    def sent(self):
        self.out.wait_send()


def kernel(
    tap_count,
    streams_hbm,
    taps_hbm,
    rates_hbm,
    residues_hbm,
    skip_hbm,
    w_hbm,
    out,
    w,
    streams,
    taps,
    rates,
    residues,
    skip,
    ext,
    query,
    gated,
    conv,
    decay,
    coef,
    rate_chunks,
    ends,
    line_in,
    row_total,
    row_in,
    part_total,
    part_in,
    enter_out,
    enter_in,
    mixed,
    total,
    load_sems,
    send_sems,
    recv_sems,
):
    poles = rates.shape[0]
    channels, tokens = streams.shape[1:]
    half = channels // 2
    rows = w_hbm.shape[0]
    ctx, tp = lax.axis_index("ctx"), lax.axis_index("tp")
    ctx_n, tp_n = lax.axis_size("ctx"), lax.axis_size("tp")
    core = ctx % 2
    x = (ctx // 2) % NX
    z = (ctx // LINE) % NZ
    y = ctx // (LINE * NZ)
    place = ctx % LINE

    def at(y_=None, z_=None, x_=None, core_=None):
        y_ = y if y_ is None else y_
        z_ = z if z_ is None else z_
        x_ = x if x_ is None else x_
        core_ = core if core_ is None else core_
        return (((y_ * NZ + z_) * NX + x_) * 2 + core_, tp)

    def flip(value, bits):
        result = value * 0
        for bit in (1, 2, 4):
            digit = (value // bit) % 2
            result = result + bit * ((1 - digit) if bits & bit else digit)
        return result

    sems = (send_sems, recv_sems)
    count = [0]
    sent = []

    def message(src, dst, land, to):
        made = Message(sems, count[0], src, dst, land, to)
        count[0] += 1
        return made

    def start_all(pair):
        for made in pair:
            made.start()
            sent.append(made)

    def recv_all(pair):
        for made in pair:
            made.recv()

    barrier = pltpu.get_barrier_semaphore()

    def greet(peer):
        pl.semaphore_signal(barrier, inc=1, device_id=peer, device_id_type=pl.DeviceIdType.MESH)

    always = [at(y_=1 - y)]
    always += [(ctx - place + flip(place, m), tp) for m in range(1, LINE)]
    always += [at(z_=flip(z, m)) for m in range(1, NZ)]
    sometimes = [
        (ctx < ctx_n - 1, (ctx + 1, tp)),
        (ctx > 0, (ctx - 1, tp)),
        (tp < tp_n - 1, (ctx, tp + 1)),
        (tp > 0, (ctx, tp - 1)),
    ]
    greetings = len(always)
    for peer in always:
        greet(peer)
    for there, peer in sometimes:
        pl.when(there)(functools.partial(greet, peer))
        greetings = greetings + there.astype(jnp.int32)

    loads = [
        pltpu.make_async_copy(src, dst, load_sems.at[n])
        for n, (src, dst) in enumerate(
            [
                (w_hbm, w.at[y, 0, x, core]),
                (streams_hbm, streams),
                (rates_hbm, rates),
                (residues_hbm, residues),
                (taps_hbm, taps),
                (skip_hbm, skip),
            ]
        )
    ]
    for load in loads:
        load.start()

    groups = [(0, 1), (1, 2), (3, 2), (5, 2), (7, 1)]
    ups, downs = at(z_=(z + 1) % NZ), at(z_=(z + NZ - 1) % NZ)
    rights, lefts = at(x_=(x + 1) % NX), at(x_=(x + NX - 1) % NX)
    x_left, x_right = (x + NX - 1) % NX, (x + 1) % NX
    x_far = (x + 2) % NX
    sibling = at(core_=1 - core)
    top, bottom = pl.ds(0, rows // 2), pl.ds(rows // 2, rows // 2)
    own, other = y, 1 - y

    across = (message(w.at[own, 0, x, core], w.at[own, 0, x, core], w.at[other, 0, x, core], at(y_=other)),)

    def za(step):
        up_src, down_src = max(2 * step - 2, 0), max(2 * step - 3, 0)
        if step < 4:
            up_dst, down_dst = w.at[other, 2 * step, x, core], w.at[other, 2 * step - 1, x, core]
            return (
                message(w.at[other, up_src, x, core], up_dst, up_dst, ups),
                message(w.at[other, down_src, x, core], down_dst, down_dst, downs),
            )
        up_dst, down_dst = w.at[other, 7, x, core, top], w.at[other, 7, x, core, bottom]
        return (
            message(w.at[other, 6, x, core, top], up_dst, up_dst, ups),
            message(w.at[other, 5, x, core, bottom], down_dst, down_dst, downs),
        )

    def xa(y_, group):
        slots = pl.ds(*groups[group])
        mine = w.at[y_, slots, x, core]
        return (
            message(mine, mine, w.at[y_, slots, x_left, core], rights),
            message(mine, mine, w.at[y_, slots, x_right, core], lefts),
        )

    def xa_far(y_, group):
        slots = pl.ds(*groups[group])
        from_left = w.at[y_, slots, x_left, core, top]
        from_right = w.at[y_, slots, x_right, core, bottom]
        return (
            message(from_left, from_left, w.at[y_, slots, x_far, core, top], rights),
            message(from_right, from_right, w.at[y_, slots, x_far, core, bottom], lefts),
        )

    def zb(step, x_, far_up):
        up_src, down_src = max(2 * step - 2, 0), max(2 * step - 3, 0)
        up_dst, down_dst = min(2 * step, 7), 2 * step - 1
        pair = ()
        if step < 4 or far_up:
            dst = w.at[own, up_dst, x_, core]
            pair += (message(w.at[own, up_src, x_, core], dst, dst, ups),)
        if step < 4 or not far_up:
            dst = w.at[own, down_dst, x_, core]
            pair += (message(w.at[own, down_src, x_, core], dst, dst, downs),)
        return pair

    def share(y_, group):
        slots = pl.ds(*groups[group])
        mine = w.at[y_, slots, pl.ds(0, NX), core]
        return (message(mine, mine, w.at[y_, slots, pl.ds(0, NX), 1 - core], sibling),)

    za_m = {s: za(s) for s in (1, 2, 3, 4)}
    xa_m = {g: xa(other, g) for g in range(5)}
    xaf_m = {g: xa_far(other, g) for g in range(5)}
    xb_m, xbf_m = xa(own, 0), xa_far(own, 0)
    chains = {"mine": (x, True), "left": (x_left, True), "right": (x_right, False), "far": (x_far, False)}
    zb_m = {(c, s): zb(s, *chains[c]) for c in chains for s in (1, 2, 3, 4)}
    own_share = {g: share(own, g) for g in range(5)}
    other_share = {g: share(other, g) for g in range(5)}

    def zb_next(chain, step):
        recv_all(zb_m[chain, step])
        start_all(zb_m[chain, step + 1])

    rim_m = message(ext.at[:, pl.ds(tokens, RIM), :], ext.at[:, pl.ds(0, RIM), :], ext.at[:, pl.ds(0, RIM), :], (ctx + 1, tp))
    eye = (
        lax.broadcasted_iota(jnp.int32, (tokens, tokens), 0)
        == lax.broadcasted_iota(jnp.int32, (tokens, tokens), 1)
    ).astype(jnp.bfloat16)
    loads[0].wait()
    loads[1].wait()
    for s in range(3):
        ext[s, pl.ds(RIM, tokens), :] = lax.dot_general(
            eye, streams[s], (((1,), (1,)), ((), ())), preferred_element_type=jnp.float32
        )
    pl.semaphore_wait(barrier, greetings)

    pl.when(ctx < ctx_n - 1)(rim_m.start)
    start_all(xb_m)
    start_all(zb_m["mine", 1])
    start_all(across)

    for load in loads[2:]:
        load.wait()
    group_count = rates.shape[1]
    spread = (
        lax.broadcasted_iota(jnp.int32, (group_count, channels), 1) // (channels // group_count)
        == lax.broadcasted_iota(jnp.int32, (group_count, channels), 0)
    ).astype(jnp.float32)
    plain = (((1,), (0,)), ((), ()))
    rate = lax.dot_general(rates[...], spread, plain, precision=HIGHEST, preferred_element_type=jnp.float32)
    residue = lax.dot_general(residues[...], spread, plain, precision=HIGHEST, preferred_element_type=jnp.float32)
    decay[...] = jnp.exp(-rate)
    coef[...] = residue * jnp.sqrt(2.0 * rate) * (1.0 / math.sqrt(poles))
    for k in range(LINE):
        rate_chunks[k] = rate[:, k * LANES : (k + 1) * LANES]

    def short_rows(first, length):
        def short(k, carry):
            lanes = pl.ds(pl.multiple_of(k * LANES, LANES), LANES)

            def filtered(s):
                total_ = None
                for shift in range(tap_count):
                    term = taps[s, pl.ds(shift, 1), lanes] * ext[s, pl.ds(RIM + first - shift, length), lanes]
                    total_ = term if total_ is None else total_ + term
                return total_

            at_rows = pl.ds(first, length)
            query[at_rows, lanes] = filtered(0)
            gated[at_rows, lanes] = (filtered(1) * filtered(2)).astype(jnp.bfloat16).astype(jnp.float32)
            return carry

        lax.fori_loop(0, channels // LANES, short, 0)

    unroll = 8

    def run_states(first, length, lanes, state):
        fall = decay[:, lanes]

        def step(t, state):
            for u in range(unroll):
                state = state * fall + gated[pl.ds(first + t * unroll + u, 1), lanes]
            return state

        return lax.fori_loop(0, length // unroll, step, state)

    short_rows(RIM, tokens - RIM)
    halves = [pl.ds(h * half, half) for h in range(2)]
    zeros = jnp.zeros((poles, half), jnp.float32)
    for h in range(2):
        state = run_states(RIM, tokens - RIM, halves[h], zeros)
        for k in range(half // LANES):
            ends[h * (half // LANES) + k] = state[:, k * LANES : (k + 1) * LANES]

    @pl.when(ctx > 0)
    def _():
        rim_m.recv()

    @pl.when(ctx == 0)
    def _():
        for s in range(3):
            ext[s, pl.ds(0, RIM), :] = jnp.zeros((RIM, channels), jnp.float32)

    short_rows(0, RIM)
    for h in range(2):
        state = run_states(0, RIM, halves[h], zeros)
        for k in range(half // LANES):
            n = h * (half // LANES) + k
            ends[n] += state[:, k * LANES : (k + 1) * LANES] * jnp.exp(rate_chunks[n] * (-float(tokens - RIM)))

    round1 = []
    for m in range(1, LINE):
        to = flip(place, m)
        round1.append(message(ends.at[to], line_in.at[place], line_in.at[to], (ctx - place + to, tp)))
    start_all(round1)
    line_in[place] = ends[place]

    recv_all(xb_m)
    start_all(xbf_m)
    start_all(zb_m["left", 1])
    start_all(zb_m["right", 1])
    zb_next("mine", 1)

    recv_all(round1)
    my_rate = rate_chunks[place]
    block_fall = jnp.exp(my_rate * (-float(tokens)))
    row_fall = jnp.exp(my_rate * (-float(tokens * LINE)))
    state = line_in[0]
    for p in range(1, LINE):
        state = state * block_fall + line_in[p]
    row_total[...] = state
    row_in[z] = state

    round2 = []
    for m in range(1, NZ):
        to = flip(z, m)
        round2.append(message(row_total, row_in.at[z], row_in.at[to], at(z_=to)))
    start_all(round2)

    recv_all(xbf_m)
    start_all(zb_m["far", 1])
    recv_all(across)
    start_all(za_m[1])
    start_all(xa_m[0])
    zb_next("mine", 2)

    recv_all(round2)
    onward = message(part_total, part_in, part_in, at(y_=1 - y))

    @pl.when(y == 0)
    def _():
        state = row_in[0]
        for r in range(1, NZ):
            state = state * row_fall + row_in[r]
        part_total[...] = state
        onward.start()
        part_in[...] = jnp.zeros_like(part_in)

    zb_next("left", 1)
    zb_next("right", 1)
    recv_all(za_m[1])
    start_all(za_m[2])
    start_all(xa_m[1])
    recv_all(xa_m[0])
    start_all(xaf_m[0])
    zb_next("far", 1)

    @pl.when(y == 1)
    def _():
        onward.recv()

    state = part_in[...]
    for r in range(NZ - 1):
        state = jnp.where(r < z, state * row_fall + row_in[r], state)
    for p in range(LINE):
        enter_out[p] = state
        if p < LINE - 1:
            state = state * block_fall + line_in[p]

    round3 = []
    for m in range(1, LINE):
        to = flip(place, m)
        round3.append(message(enter_out.at[to], enter_in.at[place], enter_in.at[to], (ctx - place + to, tp)))
    start_all(round3)
    enter_in[place] = enter_out[place]

    recv_all(za_m[2])
    start_all(za_m[3])
    start_all(xa_m[2])
    zb_next("mine", 3)
    zb_next("left", 2)
    zb_next("right", 2)
    recv_all(xa_m[1])
    start_all(xaf_m[1])

    recv_all(round3)

    right_m, left_m = {}, {}
    for h in range(2):
        for d in range(3):
            behind, ahead = (tp + tp_n - d) % tp_n, (tp + d) % tp_n
            right_m[h, d] = message(
                mixed.at[h, behind], mixed.at[h, behind], mixed.at[h, (tp + tp_n - 1 - d) % tp_n], (ctx, (tp + 1) % tp_n)
            )
            left_m[h, d] = message(
                mixed.at[h, ahead], mixed.at[h, ahead], mixed.at[h, (tp + 1 + d) % tp_n], (ctx, (tp + tp_n - 1) % tp_n)
            )

    def line_send(h, d):
        pl.when((tp < tp_n - 1) & (tp >= d))(right_m[h, d].start)
        pl.when((tp > 0) & (tp + d < tp_n))(left_m[h, d].start)

    def line_sent(h, d):
        pl.when((tp < tp_n - 1) & (tp >= d))(right_m[h, d].sent)
        pl.when((tp > 0) & (tp + d < tp_n))(left_m[h, d].sent)

    def line_recv(h, d):
        pl.when(tp >= d + 1)(right_m[h, d].recv)
        pl.when(tp + d + 1 < tp_n)(left_m[h, d].recv)

    for h in range(2):
        lanes = halves[h]
        fall, gain = decay[:, lanes], coef[:, lanes]
        first = h * (half // LANES)
        enter = jnp.concatenate([enter_in[first + k] for k in range(half // LANES)], axis=1)

        def step(t, state):
            for u in range(unroll):
                at_t = pl.ds(t * unroll + u, 1)
                state = state * fall + gated[at_t, lanes]
                conv[at_t, lanes] = jnp.sum(state * gain, axis=0, keepdims=True)
            return state

        lax.fori_loop(0, tokens // unroll, step, enter)
        mixed[h, tp] = (
            query[:, lanes] * (conv[:, lanes] + skip[:, lanes] * gated[:, lanes])
        ).astype(jnp.bfloat16)
        line_send(h, 0)

    recv_all(za_m[3])
    start_all(za_m[4])
    start_all(xa_m[3])
    zb_next("far", 2)
    zb_next("left", 3)
    zb_next("right", 3)
    recv_all(xa_m[2])
    start_all(xaf_m[2])
    start_all(own_share[0])
    start_all(own_share[1])
    start_all(own_share[2])
    line_recv(0, 0)
    line_send(0, 1)
    recv_all(za_m[4])
    start_all(xa_m[4])
    zb_next("far", 3)
    start_all(own_share[3])
    line_recv(1, 0)
    line_send(1, 1)
    recv_all(xa_m[3])
    start_all(xaf_m[3])
    for g in range(3):
        recv_all(xaf_m[g])
        start_all(other_share[g])
    line_recv(0, 1)
    line_send(0, 2)
    recv_all(xa_m[4])
    start_all(xaf_m[4])
    for c in chains:
        recv_all(zb_m[c, 4])
    start_all(own_share[4])
    line_recv(1, 1)
    line_send(1, 2)
    for g in range(3, 5):
        recv_all(xaf_m[g])
        start_all(other_share[g])
    for g in range(5):
        recv_all(own_share[g])
        recv_all(other_share[g])

    deep = LINE * rows

    def project(h, block):
        def step(k, carry):
            place_ = block * 4 + h * 2 + k
            y_, z_ = place_ // NZ, place_ % NZ
            behind = (z_ + NZ - z) % NZ
            slot = jnp.where(behind <= 4, jnp.maximum(2 * behind - 1, 0), 2 * (NZ - behind))
            weights = w[y_, slot].reshape(deep, w.shape[-1])
            part = pl.ds(pl.multiple_of(k * deep, deep), deep)
            total[...] += jnp.dot(mixed[h, block, :, part], weights, preferred_element_type=jnp.float32)
            return carry

        lax.fori_loop(0, 2, step, 0)

    total[...] = jnp.zeros_like(total)
    for h in range(2):
        project(h, tp)
    for d in range(3):
        for h in range(2):
            if d == 2:
                line_recv(h, d)

            @pl.when(tp >= d + 1)
            def _():
                project(h, tp - 1 - d)

            @pl.when(tp + d + 1 < tp_n)
            def _():
                project(h, tp + 1 + d)

    out[...] = total[...].astype(jnp.bfloat16)

    for made in sent:
        made.sent()
    pl.when(ctx < ctx_n - 1)(rim_m.sent)
    pl.when(y == 0)(onward.sent)
    for h in range(2):
        for d in range(3):
            line_sent(h, d)


def local(streams, conv_weight, rates, residues, skip, out_weight):
    channels, tokens = streams.shape[1:]
    groups, poles = rates.shape
    rows, features = out_weight.shape
    anywhere = pl.BlockSpec(memory_space=pl.ANY)
    f32, bf16 = jnp.float32, jnp.bfloat16
    messages = 1 + 8 + 20 + 4 + 28 + 10 + 1 + 7 + 7 + 1 + 7 + 12
    return pl.pallas_call(
        functools.partial(kernel, conv_weight.shape[1]),
        out_shape=jax.ShapeDtypeStruct((tokens, features), bf16),
        in_specs=[anywhere] * 6,
        out_specs=pl.BlockSpec(memory_space=pltpu.VMEM),
        scratch_shapes=[
            pltpu.VMEM((2, NZ, NX, 2, rows, features), bf16),
            pltpu.VMEM(streams.shape, bf16),
            pltpu.VMEM(conv_weight.shape, f32),
            pltpu.VMEM((poles, groups), f32),
            pltpu.VMEM((poles, groups), f32),
            pltpu.VMEM((1, channels), f32),
            pltpu.VMEM((3, RIM + tokens, channels), f32),
            pltpu.VMEM((tokens, channels), f32),
            pltpu.VMEM((tokens, channels), f32),
            pltpu.VMEM((tokens, channels), f32),
            pltpu.VMEM((poles, channels), f32),
            pltpu.VMEM((poles, channels), f32),
            pltpu.VMEM((LINE, poles, LANES), f32),
            pltpu.VMEM((LINE, poles, LANES), f32),
            pltpu.VMEM((LINE, poles, LANES), f32),
            pltpu.VMEM((poles, LANES), f32),
            pltpu.VMEM((NZ, poles, LANES), f32),
            pltpu.VMEM((poles, LANES), f32),
            pltpu.VMEM((poles, LANES), f32),
            pltpu.VMEM((LINE, poles, LANES), f32),
            pltpu.VMEM((LINE, poles, LANES), f32),
            pltpu.VMEM((2, 4, tokens, channels // 2), bf16),
            pltpu.VMEM((tokens, features), f32),
            pltpu.SemaphoreType.DMA((6,)),
            pltpu.SemaphoreType.DMA((messages,)),
            pltpu.SemaphoreType.DMA((messages,)),
        ],
        compiler_params=pltpu.CompilerParams(
            collective_id=0, has_side_effects=True, vmem_limit_bytes=60 * 1024 * 1024
        ),
        cost_estimate=pl.CostEstimate(
            flops=2 * tokens * 4 * channels * features, bytes_accessed=12 << 20, transcendentals=1 << 15
        ),
    )(streams, conv_weight, rates.T, residues.T, skip.reshape(1, channels), out_weight)


def solution(mesh):
    return jax.shard_map(
        local,
        mesh=mesh,
        in_specs=(
            P(None, "tp", "ctx"),
            P(None, None, "tp"),
            P("tp", None),
            P("tp", None),
            P("tp"),
            P("ctx", "tp"),
        ),
        out_specs=P("ctx", "tp"),
        check_vma=False,
    )
```

```python
import functools
import math

import jax
import jax.numpy as jnp
from jax import lax
from jax.experimental import pallas as pl
from jax.experimental.pallas import tpu as pltpu
from jax.sharding import PartitionSpec as P

NZ, NX = 8, 4
LINE = NX * 2
LANES = 128
RIM = 8
HIGHEST = lax.Precision.HIGHEST


class Message:
    def __init__(self, sems, number, src, dst, land, to):
        send, recv = sems
        make = functools.partial(
            pltpu.make_async_remote_copy,
            send_sem=send.at[number],
            recv_sem=recv.at[number],
            device_id=to,
            device_id_type=pl.DeviceIdType.MESH,
        )
        self.out = make(src_ref=src, dst_ref=dst)
        self.into = make(src_ref=src, dst_ref=land)

    def start(self):
        self.out.start()

    def recv(self):
        self.into.wait_recv()

    def sent(self):
        self.out.wait_send()


def kernel(
    tap_count,
    streams_hbm,
    taps_hbm,
    rates_hbm,
    residues_hbm,
    skip_hbm,
    w_hbm,
    out,
    w,
    streams,
    taps,
    rates,
    residues,
    skip,
    ext,
    query,
    gated,
    conv,
    factors,
    decay,
    coef,
    rate_chunks,
    ends,
    line_in,
    row_total,
    row_in,
    part_total,
    part_in,
    enter_out,
    enter_in,
    mixed,
    outbox,
    part_out,
    part_back,
    total,
    load_sems,
    send_sems,
    recv_sems,
):
    poles = rates.shape[0]
    channels, tokens = streams.shape[1:]
    half = channels // 2
    rows = w_hbm.shape[0]
    ctx, tp = lax.axis_index("ctx"), lax.axis_index("tp")
    ctx_n, tp_n = lax.axis_size("ctx"), lax.axis_size("tp")
    core = ctx % 2
    x = (ctx // 2) % NX
    z = (ctx // LINE) % NZ
    y = ctx // (LINE * NZ)
    place = ctx % LINE

    def at(y_=None, z_=None, x_=None, core_=None):
        y_ = y if y_ is None else y_
        z_ = z if z_ is None else z_
        x_ = x if x_ is None else x_
        core_ = core if core_ is None else core_
        return (((y_ * NZ + z_) * NX + x_) * 2 + core_, tp)

    def flip(value, bits):
        result = value * 0
        for bit in (1, 2, 4):
            digit = (value // bit) % 2
            result = result + bit * ((1 - digit) if bits & bit else digit)
        return result

    sems = (send_sems, recv_sems)
    count = [0]
    sent = []

    def message(src, dst, land, to):
        made = Message(sems, count[0], src, dst, land, to)
        count[0] += 1
        return made

    def start_all(pair):
        for made in pair:
            made.start()
            sent.append(made)

    def recv_all(pair):
        for made in pair:
            made.recv()

    barrier = pltpu.get_barrier_semaphore()

    def greet(peer):
        pl.semaphore_signal(barrier, inc=1, device_id=peer, device_id_type=pl.DeviceIdType.MESH)

    sibling = at(core_=1 - core)[0]
    always = [at(y_=1 - y)]
    always += [at(z_=flip(z, m)) for m in range(NZ - 1, 0, -1)]
    always += [(ctx - place + flip(place, m), tp) for m in range(LINE - 1, 0, -1)]
    sometimes = [
        (ctx < ctx_n - 1, (ctx + 1, tp)),
        (ctx > 0, (ctx - 1, tp)),
        (tp < tp_n - 1, (ctx, tp + 1)),
        (tp > 0, (ctx, tp - 1)),
        (tp < tp_n - 1, (sibling, tp + 1)),
        (tp > 0, (sibling, tp - 1)),
    ]
    greetings = len(always)
    for peer in always:
        greet(peer)
    for there, peer in sometimes:
        pl.when(there)(functools.partial(greet, peer))
        greetings = greetings + there.astype(jnp.int32)

    loads = [
        pltpu.make_async_copy(src, dst, load_sems.at[n])
        for n, (src, dst) in enumerate(
            [
                (w_hbm, w.at[y, 0, x, core]),
                (streams_hbm, streams),
                (rates_hbm, rates),
                (residues_hbm, residues),
                (taps_hbm, taps),
                (skip_hbm, skip),
            ]
        )
    ]
    for load in loads:
        load.start()

    groups = [(0, 1), (1, 2), (3, 2), (5, 2), (7, 1)]
    ups, downs = at(z_=(z + 1) % NZ), at(z_=(z + NZ - 1) % NZ)
    rights, lefts = at(x_=(x + 1) % NX), at(x_=(x + NX - 1) % NX)
    x_left, x_right = (x + NX - 1) % NX, (x + 1) % NX
    x_far = (x + 2) % NX
    top, bottom = pl.ds(0, rows // 2), pl.ds(rows // 2, rows // 2)
    own, other = y, 1 - y

    across = (message(w.at[own, 0, x, core], w.at[own, 0, x, core], w.at[other, 0, x, core], at(y_=other)),)

    def za(step):
        up_src, down_src = max(2 * step - 2, 0), max(2 * step - 3, 0)
        if step < 4:
            up_dst, down_dst = w.at[other, 2 * step, x, core], w.at[other, 2 * step - 1, x, core]
            return (
                message(w.at[other, up_src, x, core], up_dst, up_dst, ups),
                message(w.at[other, down_src, x, core], down_dst, down_dst, downs),
            )
        up_dst, down_dst = w.at[other, 7, x, core, top], w.at[other, 7, x, core, bottom]
        return (
            message(w.at[other, 6, x, core, top], up_dst, up_dst, ups),
            message(w.at[other, 5, x, core, bottom], down_dst, down_dst, downs),
        )

    def xa(y_, group):
        slots = pl.ds(*groups[group])
        mine = w.at[y_, slots, x, core]
        return (
            message(mine, mine, w.at[y_, slots, x_left, core], rights),
            message(mine, mine, w.at[y_, slots, x_right, core], lefts),
        )

    def xa_far(y_, group):
        slots = pl.ds(*groups[group])
        from_left = w.at[y_, slots, x_left, core, top]
        from_right = w.at[y_, slots, x_right, core, bottom]
        return (
            message(from_left, from_left, w.at[y_, slots, x_far, core, top], rights),
            message(from_right, from_right, w.at[y_, slots, x_far, core, bottom], lefts),
        )

    def zb(step, x_, far_up):
        up_src, down_src = max(2 * step - 2, 0), max(2 * step - 3, 0)
        up_dst, down_dst = min(2 * step, 7), 2 * step - 1
        pair = ()
        if step < 4 or far_up:
            dst = w.at[own, up_dst, x_, core]
            pair += (message(w.at[own, up_src, x_, core], dst, dst, ups),)
        if step < 4 or not far_up:
            dst = w.at[own, down_dst, x_, core]
            pair += (message(w.at[own, down_src, x_, core], dst, dst, downs),)
        return pair

    za_m = {s: za(s) for s in (1, 2, 3, 4)}
    xa_m = {g: xa(other, g) for g in range(5)}
    xaf_m = {g: xa_far(other, g) for g in range(5)}
    xb_m, xbf_m = xa(own, 0), xa_far(own, 0)
    chains = {"mine": (x, True), "left": (x_left, True), "right": (x_right, False), "far": (x_far, False)}
    zb_m = {(c, s): zb(s, *chains[c]) for c in chains for s in (1, 2, 3, 4)}

    def zb_next(chain, step):
        recv_all(zb_m[chain, step])
        start_all(zb_m[chain, step + 1])

    rim_m = message(ext.at[:, pl.ds(tokens, RIM), :], ext.at[:, pl.ds(0, RIM), :], ext.at[:, pl.ds(0, RIM), :], (ctx + 1, tp))
    eye = (
        lax.broadcasted_iota(jnp.int32, (tokens, tokens), 0)
        == lax.broadcasted_iota(jnp.int32, (tokens, tokens), 1)
    ).astype(jnp.bfloat16)
    loads[0].wait()
    pl.semaphore_wait(barrier, greetings)
    start_all(xb_m)
    start_all(zb_m["mine", 1])
    start_all(across)
    loads[1].wait()
    for s in range(3):
        pairs = streams[s].reshape(channels // (2 * rows), 2, rows, tokens)
        for h in range(2):
            ext[s, pl.ds(RIM, tokens), pl.ds(h * half, half)] = lax.dot_general(
                eye, pairs[:, h].reshape(half, tokens), (((1,), (1,)), ((), ())), preferred_element_type=jnp.float32
            )
    pl.when(ctx < ctx_n - 1)(rim_m.start)

    def channel_at(lane, half_width):
        return (lane % half_width) // rows * (2 * rows) + lane // half_width * rows + lane % rows

    for load in loads[2:]:
        load.wait()
    group_count = rates.shape[1]
    lane = lax.broadcasted_iota(jnp.int32, (group_count, channels), 1)
    spread = (
        channel_at(lane, half) // (channels // group_count)
        == lax.broadcasted_iota(jnp.int32, (group_count, channels), 0)
    ).astype(jnp.float32)
    plain = (((1,), (0,)), ((), ()))
    rate = lax.dot_general(rates[...], spread, plain, precision=HIGHEST, preferred_element_type=jnp.float32)
    residue = lax.dot_general(residues[...], spread, plain, precision=HIGHEST, preferred_element_type=jnp.float32)
    decay[...] = jnp.exp(-rate)
    two = 2 * LANES
    order = (
        channel_at(lax.broadcasted_iota(jnp.int32, (two, two), 1), LANES)
        == lax.broadcasted_iota(jnp.int32, (two, two), 0)
    ).astype(jnp.float32)
    by_tap = jnp.concatenate([taps[s] for s in range(3)] + [skip[...]], axis=0)
    for k in range(channels // two):
        moved = lax.dot_general(
            by_tap[:, k * two : (k + 1) * two], order, plain, precision=HIGHEST, preferred_element_type=jnp.float32
        )
        for h in range(2):
            factors[:, pl.ds(h * half + k * LANES, LANES)] = moved[:, h * LANES : (h + 1) * LANES]
    coef[...] = residue * jnp.sqrt(2.0 * rate) * (1.0 / math.sqrt(poles))
    for k in range(LINE):
        rate_chunks[k] = rate[:, k * LANES : (k + 1) * LANES]

    def short_rows(first, length):
        def short(k, carry):
            lanes = pl.ds(pl.multiple_of(k * LANES, LANES), LANES)

            def filtered(s):
                total_ = None
                for shift in range(tap_count):
                    term = factors[pl.ds(s * tap_count + shift, 1), lanes] * ext[s, pl.ds(RIM + first - shift, length), lanes]
                    total_ = term if total_ is None else total_ + term
                return total_

            at_rows = pl.ds(first, length)
            query[at_rows, lanes] = filtered(0)
            gated[at_rows, lanes] = (filtered(1) * filtered(2)).astype(jnp.bfloat16).astype(jnp.float32)
            return carry

        lax.fori_loop(0, channels // LANES, short, 0)

    unroll = 8

    def run_states(first, length, lanes, state):
        fall = decay[:, lanes]

        def step(t, state):
            for u in range(unroll):
                state = state * fall + gated[pl.ds(first + t * unroll + u, 1), lanes]
            return state

        return lax.fori_loop(0, length // unroll, step, state)

    short_rows(RIM, tokens - RIM)
    halves = [pl.ds(h * half, half) for h in range(2)]
    zeros = jnp.zeros((poles, half), jnp.float32)
    for h in range(2):
        state = run_states(RIM, tokens - RIM, halves[h], zeros)
        for k in range(half // LANES):
            ends[h * (half // LANES) + k] = state[:, k * LANES : (k + 1) * LANES]

    @pl.when(ctx > 0)
    def _():
        rim_m.recv()

    @pl.when(ctx == 0)
    def _():
        for s in range(3):
            ext[s, pl.ds(0, RIM), :] = jnp.zeros((RIM, channels), jnp.float32)

    short_rows(0, RIM)
    for h in range(2):
        state = run_states(0, RIM, halves[h], zeros)
        for k in range(half // LANES):
            n = h * (half // LANES) + k
            ends[n] += state[:, k * LANES : (k + 1) * LANES] * jnp.exp(rate_chunks[n] * (-float(tokens - RIM)))

    round1 = []
    for m in range(1, LINE):
        to = flip(place, m)
        round1.append(message(ends.at[to], line_in.at[place], line_in.at[to], (ctx - place + to, tp)))
    start_all(round1)
    line_in[place] = ends[place]
    my_rate = rate_chunks[place]
    block_fall = jnp.exp(my_rate * (-float(tokens)))
    row_fall = jnp.exp(my_rate * (-float(tokens * LINE)))

    recv_all(xb_m)
    start_all(xbf_m)
    start_all(zb_m["left", 1])
    start_all(zb_m["right", 1])
    zb_next("mine", 1)

    recv_all(round1)
    state = line_in[0]
    for p in range(1, LINE):
        state = state * block_fall + line_in[p]
    row_total[...] = state
    row_in[z] = state

    round2 = []
    for m in range(1, NZ):
        to = flip(z, m)
        round2.append(message(row_total, row_in.at[z], row_in.at[to], at(z_=to)))
    start_all(round2)

    recv_all(xbf_m)
    start_all(zb_m["far", 1])
    recv_all(across)
    start_all(za_m[1])
    start_all(xa_m[0])

    recv_all(round2)
    onward = message(part_total, part_in, part_in, at(y_=1 - y))

    @pl.when(y == 0)
    def _():
        state = row_in[0]
        for r in range(1, NZ):
            state = state * row_fall + row_in[r]
        part_total[...] = state
        onward.start()
        part_in[...] = jnp.zeros_like(part_in)

    zb_next("mine", 2)
    recv_all(za_m[1])
    start_all(za_m[2])
    start_all(xa_m[1])
    zb_next("left", 1)
    zb_next("right", 1)
    recv_all(xa_m[0])
    start_all(xaf_m[0])
    zb_next("far", 1)

    @pl.when(y == 1)
    def _():
        onward.recv()

    state = part_in[...]
    for r in range(NZ - 1):
        state = jnp.where(r < z, state * row_fall + row_in[r], state)
    for p in range(LINE):
        enter_out[p] = state
        if p < LINE - 1:
            state = state * block_fall + line_in[p]

    round3 = []
    for m in range(1, LINE):
        to = flip(place, m)
        round3.append(message(enter_out.at[to], enter_in.at[place], enter_in.at[to], (ctx - place + to, tp)))
    start_all(round3)
    enter_in[place] = enter_out[place]

    recv_all(za_m[2])
    start_all(za_m[3])
    start_all(xa_m[2])
    zb_next("mine", 3)
    recv_all(xa_m[1])
    start_all(xaf_m[1])
    zb_next("left", 2)
    zb_next("right", 2)

    recv_all(round3)

    right_m, left_m = {}, {}
    up_tp, down_tp = (tp + 1) % tp_n, (tp + tp_n - 1) % tp_n
    home = message(outbox, mixed.at[core, tp], mixed.at[1 - core, tp], (sibling, tp))
    for r in range(2):
        of = core if r == 0 else 1 - core
        for d in range(3):
            behind, ahead = (tp + tp_n - d) % tp_n, (tp + d) % tp_n
            from_left, from_right = mixed.at[of, (tp + tp_n - 1 - d) % tp_n], mixed.at[of, (tp + 1 + d) % tp_n]
            if (r, d) == (1, 0):
                right_m[r, d] = message(outbox, mixed.at[core, tp], from_left, (sibling, up_tp))
                left_m[r, d] = message(outbox, mixed.at[core, tp], from_right, (sibling, down_tp))
            else:
                right_m[r, d] = message(mixed.at[of, behind], mixed.at[of, behind], from_left, (ctx, up_tp))
                left_m[r, d] = message(mixed.at[of, ahead], mixed.at[of, ahead], from_right, (ctx, down_tp))

    def line_send(r, d):
        pl.when((tp < tp_n - 1) & (tp >= d))(right_m[r, d].start)
        pl.when((tp > 0) & (tp + d < tp_n))(left_m[r, d].start)

    def line_sent(r, d):
        pl.when((tp < tp_n - 1) & (tp >= d))(right_m[r, d].sent)
        pl.when((tp > 0) & (tp + d < tp_n))(left_m[r, d].sent)

    def line_recv(r, d):
        pl.when(tp >= d + 1)(right_m[r, d].recv)
        pl.when(tp + d + 1 < tp_n)(left_m[r, d].recv)

    for r in (1, 0):
        which = core if r == 0 else 1 - core
        lanes = pl.ds(pl.multiple_of(which * half, half), half)
        fall, gain = decay[:, lanes], coef[:, lanes]
        first = which * (half // LANES)
        enter = jnp.concatenate([enter_in[first + k] for k in range(half // LANES)], axis=1)

        def step(t, state):
            for u in range(unroll):
                at_t = pl.ds(t * unroll + u, 1)
                state = state * fall + gated[at_t, lanes]
                conv[at_t, :] = jnp.sum(state * gain, axis=0, keepdims=True)
            return state

        lax.fori_loop(0, tokens // unroll, step, enter)
        block = (
            query[:, lanes] * (conv[...] + factors[pl.ds(3 * tap_count, 1), lanes] * gated[:, lanes])
        ).astype(jnp.bfloat16)
        if r == 1:
            outbox[...] = block
            start_all((home,))
        else:
            mixed[core, tp] = block
        line_send(r, 0)

    recv_all(za_m[3])
    start_all(za_m[4])
    start_all(xa_m[3])
    zb_next("far", 2)
    recv_all(xa_m[2])
    start_all(xaf_m[2])
    zb_next("left", 3)
    line_recv(1, 0)
    line_send(1, 1)
    zb_next("right", 3)
    recv_all(za_m[4])
    start_all(xa_m[4])
    recv_all(xa_m[3])
    start_all(xaf_m[3])
    zb_next("far", 3)
    line_recv(0, 0)
    line_send(0, 1)
    recv_all(xa_m[4])
    start_all(xaf_m[4])
    line_recv(1, 1)
    line_send(1, 2)
    recv_all((home,))

    deep = NX * rows
    total[...] = jnp.zeros_like(total)

    def slot_of(z_):
        behind = (z_ + NZ - z) % NZ
        return jnp.where(behind <= 4, jnp.maximum(2 * behind - 1, 0), 2 * (NZ - behind))

    last_pair = ((z + NZ // 2) % NZ) // 2

    def project(distances, late):
        def step(n, carry):
            y_, pair = n // 4, n % 4
            block = y_ * 2 + pair // 2
            distance = jnp.maximum(block - tp, tp - block)
            wanted = (distance >= distances[0]) & (distance <= distances[1])
            if late is not None:
                wanted = wanted & ((pair == last_pair) if late else (pair != last_pair))

            @pl.when(wanted)
            def _():
                weights = jnp.concatenate(
                    [
                        w[y_, slot_of(2 * pair + k), pl.ds(0, NX), core].reshape(deep, w.shape[-1])
                        for k in range(2)
                    ],
                    axis=0,
                )
                part = pl.ds(pl.multiple_of((pair % 2) * 2 * deep, 2 * deep), 2 * deep)
                left = jnp.concatenate([mixed[c, block, :, part] for c in range(2)], axis=0)
                total[...] += jnp.dot(left, weights, preferred_element_type=jnp.float32)

            return carry

        lax.fori_loop(0, 2 * NZ // 2, step, 0)

    for g in range(4):
        recv_all(xaf_m[g])
    project((0, 0), False)
    line_recv(0, 1)
    line_send(0, 2)
    project((1, 2), False)
    recv_all(xaf_m[4])
    for c in chains:
        recv_all(zb_m[c, 4])
    project((0, 2), True)
    line_recv(1, 2)
    line_recv(0, 2)
    project((3, 3), None)

    part_out[...] = total[pl.ds(pl.multiple_of((1 - core) * tokens, tokens), tokens), :].astype(jnp.bfloat16)
    swap = message(part_out, part_back, part_back, (sibling, tp))
    start_all((swap,))
    recv_all((swap,))
    mine = total[pl.ds(pl.multiple_of(core * tokens, tokens), tokens), :]
    out[...] = (mine + part_back[...].astype(jnp.float32)).astype(jnp.bfloat16)

    for made in sent:
        made.sent()
    pl.when(ctx < ctx_n - 1)(rim_m.sent)
    pl.when(y == 0)(onward.sent)
    for r in range(2):
        for d in range(3):
            line_sent(r, d)


def local(streams, conv_weight, rates, residues, skip, out_weight):
    channels, tokens = streams.shape[1:]
    groups, poles = rates.shape
    rows, features = out_weight.shape
    anywhere = pl.BlockSpec(memory_space=pl.ANY)
    f32, bf16 = jnp.float32, jnp.bfloat16
    messages = 1 + 8 + 20 + 4 + 28 + 1 + 7 + 7 + 1 + 7 + 13 + 1
    return pl.pallas_call(
        functools.partial(kernel, conv_weight.shape[1]),
        out_shape=jax.ShapeDtypeStruct((tokens, features), bf16),
        in_specs=[anywhere] * 6,
        out_specs=pl.BlockSpec(memory_space=pltpu.VMEM),
        scratch_shapes=[
            pltpu.VMEM((2, NZ, NX, 2, rows, features), bf16),
            pltpu.VMEM(streams.shape, bf16),
            pltpu.VMEM(conv_weight.shape, f32),
            pltpu.VMEM((poles, groups), f32),
            pltpu.VMEM((poles, groups), f32),
            pltpu.VMEM((1, channels), f32),
            pltpu.VMEM((3, RIM + tokens, channels), f32),
            pltpu.VMEM((tokens, channels), f32),
            pltpu.VMEM((tokens, channels), f32),
            pltpu.VMEM((tokens, channels // 2), f32),
            pltpu.VMEM((3 * conv_weight.shape[1] + 1, channels), f32),
            pltpu.VMEM((poles, channels), f32),
            pltpu.VMEM((poles, channels), f32),
            pltpu.VMEM((LINE, poles, LANES), f32),
            pltpu.VMEM((LINE, poles, LANES), f32),
            pltpu.VMEM((LINE, poles, LANES), f32),
            pltpu.VMEM((poles, LANES), f32),
            pltpu.VMEM((NZ, poles, LANES), f32),
            pltpu.VMEM((poles, LANES), f32),
            pltpu.VMEM((poles, LANES), f32),
            pltpu.VMEM((LINE, poles, LANES), f32),
            pltpu.VMEM((LINE, poles, LANES), f32),
            pltpu.VMEM((2, 4, tokens, channels // 2), bf16),
            pltpu.VMEM((tokens, channels // 2), bf16),
            pltpu.VMEM((tokens, features), bf16),
            pltpu.VMEM((tokens, features), bf16),
            pltpu.VMEM((2 * tokens, features), f32),
            pltpu.SemaphoreType.DMA((6,)),
            pltpu.SemaphoreType.DMA((messages,)),
            pltpu.SemaphoreType.DMA((messages,)),
        ],
        compiler_params=pltpu.CompilerParams(
            collective_id=0, has_side_effects=True, vmem_limit_bytes=60 * 1024 * 1024
        ),
        cost_estimate=pl.CostEstimate(
            flops=2 * tokens * 4 * channels * features, bytes_accessed=12 << 20, transcendentals=1 << 15
        ),
    )(streams, conv_weight, rates.T, residues.T, skip.reshape(1, channels), out_weight)


def solution(mesh):
    return jax.shard_map(
        local,
        mesh=mesh,
        in_specs=(
            P(None, "tp", "ctx"),
            P(None, None, "tp"),
            P("tp", None),
            P("tp", None),
            P("tp"),
            P("ctx", "tp"),
        ),
        out_specs=P("ctx", "tp"),
        check_vma=False,
    )
```

```python
import functools
import math

import jax
import jax.numpy as jnp
from jax import lax
from jax.experimental import pallas as pl
from jax.experimental.pallas import tpu as pltpu
from jax.sharding import PartitionSpec as P

NZ, NX = 8, 4
LINE = NX * 2
LANES = 128
RIM = 8
HIGHEST = lax.Precision.HIGHEST


class Message:
    def __init__(self, sems, number, src, dst, land, to):
        send, recv = sems
        make = functools.partial(
            pltpu.make_async_remote_copy,
            send_sem=send.at[number],
            recv_sem=recv.at[number],
            device_id=to,
            device_id_type=pl.DeviceIdType.MESH,
        )
        self.out = make(src_ref=src, dst_ref=dst)
        self.into = make(src_ref=src, dst_ref=land)

    def start(self):
        self.out.start()

    def recv(self):
        self.into.wait_recv()

    def sent(self):
        self.out.wait_send()


def kernel(
    tap_count,
    streams_hbm,
    taps_hbm,
    rates_hbm,
    residues_hbm,
    skip_hbm,
    w_hbm,
    out,
    w,
    streams,
    taps,
    rates,
    residues,
    skip,
    ext,
    query,
    gated,
    conv,
    factors,
    decay,
    coef,
    rate_chunks,
    ends,
    line_in,
    row_total,
    row_in,
    part_total,
    part_in,
    enter_out,
    enter_in,
    mixed,
    outbox,
    part_out,
    part_back,
    total,
    heard,
    load_sems,
    send_sems,
    recv_sems,
):
    poles = rates.shape[0]
    channels, tokens = streams.shape[1:]
    half = channels // 2
    rows = w_hbm.shape[0]
    ctx, tp = lax.axis_index("ctx"), lax.axis_index("tp")
    ctx_n, tp_n = lax.axis_size("ctx"), lax.axis_size("tp")
    core = ctx % 2
    x = (ctx // 2) % NX
    z = (ctx // LINE) % NZ
    y = ctx // (LINE * NZ)
    place = ctx % LINE

    def at(y_=None, z_=None, x_=None, core_=None):
        y_ = y if y_ is None else y_
        z_ = z if z_ is None else z_
        x_ = x if x_ is None else x_
        core_ = core if core_ is None else core_
        return (((y_ * NZ + z_) * NX + x_) * 2 + core_, tp)

    def flip(value, bits):
        result = value * 0
        for bit in (1, 2, 4):
            digit = (value // bit) % 2
            result = result + bit * ((1 - digit) if bits & bit else digit)
        return result

    sems = (send_sems, recv_sems)
    count = [0]
    sent = []

    def message(src, dst, land, to):
        made = Message(sems, count[0], src, dst, land, to)
        count[0] += 1
        return made

    def start_all(pair):
        for made in pair:
            made.start()
            sent.append(made)

    def recv_all(pair):
        for made in pair:
            made.recv()

    barrier = pltpu.get_barrier_semaphore()

    def greet(peer):
        pl.semaphore_signal(barrier, inc=1, device_id=peer, device_id_type=pl.DeviceIdType.MESH)

    sibling = at(core_=1 - core)[0]
    ups, downs = at(z_=(z + 1) % NZ), at(z_=(z + NZ - 1) % NZ)
    wraps_up, wraps_down = tp == tp_n - 1, tp == 0
    crossed = (ctx + ctx_n // 2) % ctx_n
    onwards = (jnp.where(wraps_up, crossed, ctx), jnp.where(wraps_up, 0, tp + 1))
    backwards = (jnp.where(wraps_down, crossed, ctx), jnp.where(wraps_down, tp_n - 1, tp - 1))
    always = [ups, downs, onwards, backwards]
    always += [(ctx - place + flip(place, m), tp) for m in range(LINE - 1, 0, -1)]
    for peer in always:
        greet(peer)
    pl.when(ctx > 0)(functools.partial(greet, (ctx - 1, tp)))
    pl.when(tp < tp_n - 1)(functools.partial(greet, (sibling, tp + 1)))
    pl.when(tp > 0)(functools.partial(greet, (sibling, tp - 1)))
    greetings = len(always)
    for there in (ctx < ctx_n - 1, tp < tp_n - 1, tp > 0):
        greetings = greetings + there.astype(jnp.int32)

    ways = [ups, downs, onwards]

    def tell(way, step):
        pl.semaphore_signal(
            heard.at[way, step], inc=1, device_id=ways[way], device_id_type=pl.DeviceIdType.MESH
        )

    def pass_on(step):
        for way in range(3):
            pl.semaphore_wait(heard.at[way, step], 1)
            if step < 2:
                tell(way, step + 1)

    loads = [
        pltpu.make_async_copy(src, dst, load_sems.at[n])
        for n, (src, dst) in enumerate(
            [
                (rates_hbm, rates),
                (residues_hbm, residues),
                (w_hbm, w.at[y, 0, x, core]),
                (streams_hbm, streams),
                (taps_hbm, taps),
                (skip_hbm, skip),
            ]
        )
    ]
    for load in loads:
        load.start()

    groups = [(0, 1), (1, 2), (3, 2), (5, 2), (7, 1)]
    rights, lefts = at(x_=(x + 1) % NX), at(x_=(x + NX - 1) % NX)
    x_left, x_right = (x + NX - 1) % NX, (x + 1) % NX
    x_far = (x + 2) % NX
    top, bottom = pl.ds(0, rows // 2), pl.ds(rows // 2, rows // 2)
    own, other = y, 1 - y

    across = (message(w.at[own, 0, x, core], w.at[own, 0, x, core], w.at[other, 0, x, core], at(y_=other)),)

    def za(step):
        up_src, down_src = max(2 * step - 2, 0), max(2 * step - 3, 0)
        if step < 4:
            up_dst, down_dst = w.at[other, 2 * step, x, core], w.at[other, 2 * step - 1, x, core]
            return (
                message(w.at[other, up_src, x, core], up_dst, up_dst, ups),
                message(w.at[other, down_src, x, core], down_dst, down_dst, downs),
            )
        up_dst, down_dst = w.at[other, 7, x, core, top], w.at[other, 7, x, core, bottom]
        return (
            message(w.at[other, 6, x, core, top], up_dst, up_dst, ups),
            message(w.at[other, 5, x, core, bottom], down_dst, down_dst, downs),
        )

    def xa(y_, group):
        slots = pl.ds(*groups[group])
        mine = w.at[y_, slots, x, core]
        return (
            message(mine, mine, w.at[y_, slots, x_left, core], rights),
            message(mine, mine, w.at[y_, slots, x_right, core], lefts),
        )

    def xa_far(y_, group):
        slots = pl.ds(*groups[group])
        from_left = w.at[y_, slots, x_left, core, top]
        from_right = w.at[y_, slots, x_right, core, bottom]
        return (
            message(from_left, from_left, w.at[y_, slots, x_far, core, top], rights),
            message(from_right, from_right, w.at[y_, slots, x_far, core, bottom], lefts),
        )

    def zb(step, x_, far_up):
        up_src, down_src = max(2 * step - 2, 0), max(2 * step - 3, 0)
        up_dst, down_dst = min(2 * step, 7), 2 * step - 1
        pair = ()
        if step < 4 or far_up:
            dst = w.at[own, up_dst, x_, core]
            pair += (message(w.at[own, up_src, x_, core], dst, dst, ups),)
        if step < 4 or not far_up:
            dst = w.at[own, down_dst, x_, core]
            pair += (message(w.at[own, down_src, x_, core], dst, dst, downs),)
        return pair

    za_m = {s: za(s) for s in (1, 2, 3, 4)}
    xa_m = {g: xa(other, g) for g in range(5)}
    xaf_m = {g: xa_far(other, g) for g in range(5)}
    xb_m, xbf_m = xa(own, 0), xa_far(own, 0)
    chains = {"mine": (x, True), "left": (x_left, True), "right": (x_right, False), "far": (x_far, False)}
    zb_m = {(c, s): zb(s, *chains[c]) for c in chains for s in (1, 2, 3, 4)}

    def zb_next(chain, step):
        recv_all(zb_m[chain, step])
        start_all(zb_m[chain, step + 1])

    def channel_at(lane, half_width):
        return (lane % half_width) // rows * (2 * rows) + lane // half_width * rows + lane % rows

    plain = (((1,), (0,)), ((), ()))
    group_count = rates.shape[1]
    lane = lax.broadcasted_iota(jnp.int32, (group_count, channels), 1)
    spread = (
        channel_at(lane, half) // (channels // group_count)
        == lax.broadcasted_iota(jnp.int32, (group_count, channels), 0)
    ).astype(jnp.float32)
    loads[0].wait()
    loads[1].wait()
    rate = lax.dot_general(rates[...], spread, plain, precision=HIGHEST, preferred_element_type=jnp.float32)
    residue = lax.dot_general(residues[...], spread, plain, precision=HIGHEST, preferred_element_type=jnp.float32)
    decay[...] = jnp.exp(-rate)
    coef[...] = residue * jnp.sqrt(2.0 * rate) * (1.0 / math.sqrt(poles))
    for k in range(LINE):
        rate_chunks[k] = rate[:, k * LANES : (k + 1) * LANES]

    loads[2].wait()
    pl.semaphore_wait(barrier, greetings)
    for way in range(3):
        tell(way, 0)
    start_all(xb_m)
    start_all(zb_m["mine", 1])

    rim_m = message(
        ext.at[:, pl.ds(tokens, RIM), :], ext.at[:, pl.ds(0, RIM), :], ext.at[:, pl.ds(0, RIM), :], (ctx + 1, tp)
    )
    eye = (
        lax.broadcasted_iota(jnp.int32, (tokens, tokens), 0)
        == lax.broadcasted_iota(jnp.int32, (tokens, tokens), 1)
    ).astype(jnp.bfloat16)
    loads[3].wait()
    for s in range(3):
        pairs = streams[s].reshape(channels // (2 * rows), 2, rows, tokens)
        for h in range(2):
            ext[s, pl.ds(RIM, tokens), pl.ds(h * half, half)] = lax.dot_general(
                eye, pairs[:, h].reshape(half, tokens), (((1,), (1,)), ((), ())), preferred_element_type=jnp.float32
            )
    pl.when(ctx < ctx_n - 1)(rim_m.start)
    pass_on(0)

    two = 2 * LANES
    order = (
        channel_at(lax.broadcasted_iota(jnp.int32, (two, two), 1), LANES)
        == lax.broadcasted_iota(jnp.int32, (two, two), 0)
    ).astype(jnp.float32)
    loads[4].wait()
    loads[5].wait()
    by_tap = jnp.concatenate([taps[s] for s in range(3)] + [skip[...]], axis=0)
    for k in range(channels // two):
        moved = lax.dot_general(
            by_tap[:, k * two : (k + 1) * two], order, plain, precision=HIGHEST, preferred_element_type=jnp.float32
        )
        for h in range(2):
            factors[:, pl.ds(h * half + k * LANES, LANES)] = moved[:, h * LANES : (h + 1) * LANES]

    def short_rows(first, length):
        def short(k, carry):
            lanes = pl.ds(pl.multiple_of(k * LANES, LANES), LANES)

            def filtered(s):
                total_ = None
                for shift in range(tap_count):
                    term = factors[pl.ds(s * tap_count + shift, 1), lanes] * ext[s, pl.ds(RIM + first - shift, length), lanes]
                    total_ = term if total_ is None else total_ + term
                return total_

            at_rows = pl.ds(first, length)
            query[at_rows, lanes] = filtered(0)
            gated[at_rows, lanes] = (filtered(1) * filtered(2)).astype(jnp.bfloat16).astype(jnp.float32)
            return carry

        lax.fori_loop(0, channels // LANES, short, 0)

    unroll = 8

    def run_states(first, length, lanes, state):
        fall = decay[:, lanes]

        def step(t, state):
            for u in range(unroll):
                state = state * fall + gated[pl.ds(first + t * unroll + u, 1), lanes]
            return state

        return lax.fori_loop(0, length // unroll, step, state)

    short_rows(RIM, tokens - RIM)
    pass_on(1)
    halves = [pl.ds(h * half, half) for h in range(2)]
    zeros = jnp.zeros((poles, half), jnp.float32)
    for h in range(2):
        state = run_states(RIM, tokens - RIM, halves[h], zeros)
        for k in range(half // LANES):
            ends[h * (half // LANES) + k] = state[:, k * LANES : (k + 1) * LANES]

    pass_on(2)
    start_all(across)

    @pl.when(ctx > 0)
    def _():
        rim_m.recv()

    @pl.when(ctx == 0)
    def _():
        for s in range(3):
            ext[s, pl.ds(0, RIM), :] = jnp.zeros((RIM, channels), jnp.float32)

    short_rows(0, RIM)
    for h in range(2):
        state = run_states(0, RIM, halves[h], zeros)
        for k in range(half // LANES):
            n = h * (half // LANES) + k
            ends[n] += state[:, k * LANES : (k + 1) * LANES] * jnp.exp(rate_chunks[n] * (-float(tokens - RIM)))

    round1 = []
    for m in range(1, LINE):
        to = flip(place, m)
        round1.append(message(ends.at[to], line_in.at[place], line_in.at[to], (ctx - place + to, tp)))
    start_all(round1)
    line_in[place] = ends[place]
    my_rate = rate_chunks[place]
    block_fall = jnp.exp(my_rate * (-float(tokens)))
    row_fall = jnp.exp(my_rate * (-float(tokens * LINE)))

    recv_all(xb_m)
    start_all(xbf_m)
    start_all(zb_m["left", 1])
    start_all(zb_m["right", 1])
    zb_next("mine", 1)

    recv_all(round1)
    state = line_in[0]
    for p in range(1, LINE):
        state = state * block_fall + line_in[p]
    row_total[...] = state
    row_in[z] = state

    round2 = []
    for m in range(1, NZ):
        to = flip(z, m)
        round2.append(message(row_total, row_in.at[z], row_in.at[to], at(z_=to)))
    start_all(round2)

    recv_all(xbf_m)
    start_all(zb_m["far", 1])
    recv_all(across)
    start_all(za_m[1])
    start_all(xa_m[0])

    recv_all(round2)
    onward = message(part_total, part_in, part_in, at(y_=1 - y))

    @pl.when(y == 0)
    def _():
        state = row_in[0]
        for r in range(1, NZ):
            state = state * row_fall + row_in[r]
        part_total[...] = state
        onward.start()
        part_in[...] = jnp.zeros_like(part_in)

    zb_next("mine", 2)
    recv_all(za_m[1])
    start_all(za_m[2])
    start_all(xa_m[1])
    zb_next("left", 1)
    zb_next("right", 1)
    recv_all(xa_m[0])
    start_all(xaf_m[0])
    zb_next("far", 1)

    @pl.when(y == 1)
    def _():
        onward.recv()

    state = part_in[...]
    for r in range(NZ - 1):
        state = jnp.where(r < z, state * row_fall + row_in[r], state)
    for p in range(LINE):
        enter_out[p] = state
        if p < LINE - 1:
            state = state * block_fall + line_in[p]

    round3 = []
    for m in range(1, LINE):
        to = flip(place, m)
        round3.append(message(enter_out.at[to], enter_in.at[place], enter_in.at[to], (ctx - place + to, tp)))
    start_all(round3)
    enter_in[place] = enter_out[place]

    recv_all(za_m[2])
    start_all(za_m[3])
    start_all(xa_m[2])
    zb_next("mine", 3)
    recv_all(xa_m[1])
    start_all(xaf_m[1])
    zb_next("left", 2)
    zb_next("right", 2)

    recv_all(round3)

    right_m, left_m = {}, {}
    up_tp, down_tp = (tp + 1) % tp_n, (tp + tp_n - 1) % tp_n
    home = message(outbox, mixed.at[core, tp], mixed.at[1 - core, tp], (sibling, tp))
    for r in range(2):
        of = core if r == 0 else 1 - core
        for d in range(3):
            behind, ahead = (tp + tp_n - d) % tp_n, (tp + d) % tp_n
            from_left, from_right = mixed.at[of, (tp + tp_n - 1 - d) % tp_n], mixed.at[of, (tp + 1 + d) % tp_n]
            if (r, d) == (1, 0):
                right_m[r, d] = message(outbox, mixed.at[core, tp], from_left, (sibling, up_tp))
                left_m[r, d] = message(outbox, mixed.at[core, tp], from_right, (sibling, down_tp))
            else:
                right_m[r, d] = message(mixed.at[of, behind], mixed.at[of, behind], from_left, (ctx, up_tp))
                left_m[r, d] = message(mixed.at[of, ahead], mixed.at[of, ahead], from_right, (ctx, down_tp))

    def line_send(r, d):
        pl.when((tp < tp_n - 1) & (tp >= d))(right_m[r, d].start)
        pl.when((tp > 0) & (tp + d < tp_n))(left_m[r, d].start)

    def line_sent(r, d):
        pl.when((tp < tp_n - 1) & (tp >= d))(right_m[r, d].sent)
        pl.when((tp > 0) & (tp + d < tp_n))(left_m[r, d].sent)

    def line_recv(r, d):
        pl.when(tp >= d + 1)(right_m[r, d].recv)
        pl.when(tp + d + 1 < tp_n)(left_m[r, d].recv)

    for r in (1, 0):
        which = core if r == 0 else 1 - core
        lanes = pl.ds(pl.multiple_of(which * half, half), half)
        fall, gain = decay[:, lanes], coef[:, lanes]
        first = which * (half // LANES)
        enter = jnp.concatenate([enter_in[first + k] for k in range(half // LANES)], axis=1)

        def step(t, state):
            for u in range(unroll):
                at_t = pl.ds(t * unroll + u, 1)
                state = state * fall + gated[at_t, lanes]
                conv[at_t, :] = jnp.sum(state * gain, axis=0, keepdims=True)
            return state

        lax.fori_loop(0, tokens // unroll, step, enter)
        block = (
            query[:, lanes] * (conv[...] + factors[pl.ds(3 * tap_count, 1), lanes] * gated[:, lanes])
        ).astype(jnp.bfloat16)
        if r == 1:
            outbox[...] = block
            start_all((home,))
        else:
            mixed[core, tp] = block
        line_send(r, 0)

    recv_all(za_m[3])
    start_all(za_m[4])
    start_all(xa_m[3])
    zb_next("far", 2)
    recv_all(xa_m[2])
    start_all(xaf_m[2])
    zb_next("left", 3)
    line_recv(1, 0)
    line_send(1, 1)
    zb_next("right", 3)
    recv_all(za_m[4])
    start_all(xa_m[4])
    recv_all(xa_m[3])
    start_all(xaf_m[3])
    zb_next("far", 3)
    line_recv(0, 0)
    line_send(0, 1)
    recv_all(xa_m[4])
    start_all(xaf_m[4])
    line_recv(1, 1)
    line_send(1, 2)
    recv_all((home,))

    deep = NX * rows
    total[...] = jnp.zeros_like(total)

    def slot_of(z_):
        behind = (z_ + NZ - z) % NZ
        return jnp.where(behind <= 4, jnp.maximum(2 * behind - 1, 0), 2 * (NZ - behind))

    def tokens_of(c):
        return pl.ds(pl.multiple_of(c * tokens, tokens), tokens)

    last_pair = ((z + NZ // 2) % NZ) // 2

    def project(distances, late, only=None):
        def step(n, carry):
            y_, pair = n // 4, n % 4
            block = y_ * 2 + pair // 2
            distance = jnp.maximum(block - tp, tp - block)
            wanted = (distance >= distances[0]) & (distance <= distances[1])
            if late is not None:
                wanted = wanted & ((pair == last_pair) if late else (pair != last_pair))

            @pl.when(wanted)
            def _():
                weights = jnp.concatenate(
                    [
                        w[y_, slot_of(2 * pair + k), pl.ds(0, NX), core].reshape(deep, w.shape[-1])
                        for k in range(2)
                    ],
                    axis=0,
                )
                part = pl.ds(pl.multiple_of((pair % 2) * 2 * deep, 2 * deep), 2 * deep)
                if only is None:
                    left = jnp.concatenate([mixed[c, block, :, part] for c in range(2)], axis=0)
                    total[...] += jnp.dot(left, weights, preferred_element_type=jnp.float32)
                else:
                    total[tokens_of(only), :] += jnp.dot(
                        mixed[only, block, :, part], weights, preferred_element_type=jnp.float32
                    )

            return carry

        lax.fori_loop(0, 2 * NZ // 2, step, 0)

    for g in range(4):
        recv_all(xaf_m[g])
    project((0, 0), False)
    line_recv(0, 1)
    line_send(0, 2)
    project((1, 2), False)
    recv_all(xaf_m[4])
    for c in chains:
        recv_all(zb_m[c, 4])
    project((0, 2), True)
    line_recv(1, 2)
    project((3, 3), None, 1 - core)
    part_out[...] = total[tokens_of(1 - core), :].astype(jnp.bfloat16)
    swap = message(part_out, part_back, part_back, (sibling, tp))
    start_all((swap,))
    line_recv(0, 2)
    project((3, 3), None, core)
    recv_all((swap,))
    out[...] = (total[tokens_of(core), :] + part_back[...].astype(jnp.float32)).astype(jnp.bfloat16)

    for made in sent:
        made.sent()
    pl.when(ctx < ctx_n - 1)(rim_m.sent)
    pl.when(y == 0)(onward.sent)
    for r in range(2):
        for d in range(3):
            line_sent(r, d)


def local(streams, conv_weight, rates, residues, skip, out_weight):
    channels, tokens = streams.shape[1:]
    groups, poles = rates.shape
    rows, features = out_weight.shape
    anywhere = pl.BlockSpec(memory_space=pl.ANY)
    f32, bf16 = jnp.float32, jnp.bfloat16
    messages = 1 + 8 + 20 + 4 + 28 + 1 + 7 + 7 + 1 + 7 + 13 + 1
    return pl.pallas_call(
        functools.partial(kernel, conv_weight.shape[1]),
        out_shape=jax.ShapeDtypeStruct((tokens, features), bf16),
        in_specs=[anywhere] * 6,
        out_specs=pl.BlockSpec(memory_space=pltpu.VMEM),
        scratch_shapes=[
            pltpu.VMEM((2, NZ, NX, 2, rows, features), bf16),
            pltpu.VMEM(streams.shape, bf16),
            pltpu.VMEM(conv_weight.shape, f32),
            pltpu.VMEM((poles, groups), f32),
            pltpu.VMEM((poles, groups), f32),
            pltpu.VMEM((1, channels), f32),
            pltpu.VMEM((3, RIM + tokens, channels), f32),
            pltpu.VMEM((tokens, channels), f32),
            pltpu.VMEM((tokens, channels), f32),
            pltpu.VMEM((tokens, channels // 2), f32),
            pltpu.VMEM((3 * conv_weight.shape[1] + 1, channels), f32),
            pltpu.VMEM((poles, channels), f32),
            pltpu.VMEM((poles, channels), f32),
            pltpu.VMEM((LINE, poles, LANES), f32),
            pltpu.VMEM((LINE, poles, LANES), f32),
            pltpu.VMEM((LINE, poles, LANES), f32),
            pltpu.VMEM((poles, LANES), f32),
            pltpu.VMEM((NZ, poles, LANES), f32),
            pltpu.VMEM((poles, LANES), f32),
            pltpu.VMEM((poles, LANES), f32),
            pltpu.VMEM((LINE, poles, LANES), f32),
            pltpu.VMEM((LINE, poles, LANES), f32),
            pltpu.VMEM((2, 4, tokens, channels // 2), bf16),
            pltpu.VMEM((tokens, channels // 2), bf16),
            pltpu.VMEM((tokens, features), bf16),
            pltpu.VMEM((tokens, features), bf16),
            pltpu.VMEM((2 * tokens, features), f32),
            pltpu.SemaphoreType.REGULAR((3, 3)),
            pltpu.SemaphoreType.DMA((6,)),
            pltpu.SemaphoreType.DMA((messages,)),
            pltpu.SemaphoreType.DMA((messages,)),
        ],
        compiler_params=pltpu.CompilerParams(
            collective_id=0, has_side_effects=True, vmem_limit_bytes=60 * 1024 * 1024
        ),
        cost_estimate=pl.CostEstimate(
            flops=2 * tokens * 4 * channels * features, bytes_accessed=12 << 20, transcendentals=1 << 15
        ),
    )(streams, conv_weight, rates.T, residues.T, skip.reshape(1, channels), out_weight)


def solution(mesh):
    return jax.shard_map(
        local,
        mesh=mesh,
        in_specs=(
            P(None, "tp", "ctx"),
            P(None, None, "tp"),
            P("tp", None),
            P("tp", None),
            P("tp"),
            P("ctx", "tp"),
        ),
        out_specs=P("ctx", "tp"),
        check_vma=False,
    )
```

```python
import functools
import math

import jax
import jax.numpy as jnp
from jax import lax
from jax.experimental import pallas as pl
from jax.experimental.pallas import tpu as pltpu
from jax.sharding import PartitionSpec as P

NZ, NX = 8, 4
LINE = NX * 2
LANES = 128
RIM = 8
HIGHEST = lax.Precision.HIGHEST


class Message:
    def __init__(self, sems, number, src, dst, land, to):
        send, recv = sems
        make = functools.partial(
            pltpu.make_async_remote_copy,
            send_sem=send.at[number],
            recv_sem=recv.at[number],
            device_id=to,
            device_id_type=pl.DeviceIdType.MESH,
        )
        self.out = make(src_ref=src, dst_ref=dst)
        self.into = make(src_ref=src, dst_ref=land)

    def start(self):
        self.out.start()

    def recv(self):
        self.into.wait_recv()

    def sent(self):
        self.out.wait_send()


def kernel(
    tap_count,
    streams_hbm,
    taps_hbm,
    rates_hbm,
    residues_hbm,
    skip_hbm,
    w_hbm,
    out,
    w,
    streams,
    taps,
    rates,
    residues,
    skip,
    ext,
    query,
    gated,
    conv,
    factors,
    decay,
    coef,
    rate_chunks,
    ends,
    line_in,
    row_total,
    row_in,
    part_total,
    part_in,
    since,
    enter_out,
    enter_in,
    mixed,
    outbox,
    part_out,
    part_back,
    total,
    heard,
    load_sems,
    send_sems,
    recv_sems,
):
    poles = rates.shape[0]
    channels, tokens = streams.shape[1:]
    half = channels // 2
    rows = w_hbm.shape[0]
    ctx, tp = lax.axis_index("ctx"), lax.axis_index("tp")
    ctx_n, tp_n = lax.axis_size("ctx"), lax.axis_size("tp")
    core = ctx % 2
    x = (ctx // 2) % NX
    z = (ctx // LINE) % NZ
    y = ctx // (LINE * NZ)
    place = ctx % LINE

    def at(y_=None, z_=None, x_=None, core_=None):
        y_ = y if y_ is None else y_
        z_ = z if z_ is None else z_
        x_ = x if x_ is None else x_
        core_ = core if core_ is None else core_
        return (((y_ * NZ + z_) * NX + x_) * 2 + core_, tp)

    def flip(value, bits):
        result = value * 0
        for bit in (1, 2, 4):
            digit = (value // bit) % 2
            result = result + bit * ((1 - digit) if bits & bit else digit)
        return result

    sems = (send_sems, recv_sems)
    count = [0]
    sent = []

    def message(src, dst, land, to):
        made = Message(sems, count[0], src, dst, land, to)
        count[0] += 1
        return made

    def start_all(pair):
        for made in pair:
            made.start()
            sent.append(made)

    def recv_all(pair):
        for made in pair:
            made.recv()

    barrier = pltpu.get_barrier_semaphore()

    def greet(peer):
        pl.semaphore_signal(barrier, inc=1, device_id=peer, device_id_type=pl.DeviceIdType.MESH)

    sibling = at(core_=1 - core)[0]
    ups, downs = at(z_=(z + 1) % NZ), at(z_=(z + NZ - 1) % NZ)
    wraps_up, wraps_down = tp == tp_n - 1, tp == 0
    crossed = (ctx + ctx_n // 2) % ctx_n
    onwards = (jnp.where(wraps_up, crossed, ctx), jnp.where(wraps_up, 0, tp + 1))
    backwards = (jnp.where(wraps_down, crossed, ctx), jnp.where(wraps_down, tp_n - 1, tp - 1))
    always = [ups, downs, onwards, backwards]
    always += [(ctx - place + flip(place, m), tp) for m in range(LINE - 1, 0, -1)]
    for peer in always:
        greet(peer)
    pl.when(ctx > 0)(functools.partial(greet, (ctx - 1, tp)))
    pl.when(tp < tp_n - 1)(functools.partial(greet, (sibling, tp + 1)))
    pl.when(tp > 0)(functools.partial(greet, (sibling, tp - 1)))
    greetings = len(always)
    for there in (ctx < ctx_n - 1, tp < tp_n - 1, tp > 0):
        greetings = greetings + there.astype(jnp.int32)

    ways = [ups, downs, onwards]
    last_step = [2, 2, 3]

    def tell(way, step):
        pl.semaphore_signal(
            heard.at[way, step], inc=1, device_id=ways[way], device_id_type=pl.DeviceIdType.MESH
        )

    def pass_on(step):
        for way in range(3):
            if step <= last_step[way]:
                pl.semaphore_wait(heard.at[way, step], 1)
            if step < last_step[way]:
                tell(way, step + 1)

    loads = [
        pltpu.make_async_copy(src, dst, load_sems.at[n])
        for n, (src, dst) in enumerate(
            [
                (rates_hbm, rates),
                (residues_hbm, residues),
                (w_hbm, w.at[y, 0, x, core]),
                (streams_hbm, streams),
                (taps_hbm, taps),
                (skip_hbm, skip),
            ]
        )
    ]
    for load in loads:
        load.start()

    groups = [(0, 1), (1, 2), (3, 2), (5, 2), (7, 1)]
    rights, lefts = at(x_=(x + 1) % NX), at(x_=(x + NX - 1) % NX)
    x_left, x_right = (x + NX - 1) % NX, (x + 1) % NX
    x_far = (x + 2) % NX
    top, bottom = pl.ds(0, rows // 2), pl.ds(rows // 2, rows // 2)
    own, other = y, 1 - y

    across = (message(w.at[own, 0, x, core], w.at[own, 0, x, core], w.at[other, 0, x, core], at(y_=other)),)

    def za(step):
        up_src, down_src = max(2 * step - 2, 0), max(2 * step - 3, 0)
        if step < 4:
            up_dst, down_dst = w.at[other, 2 * step, x, core], w.at[other, 2 * step - 1, x, core]
            return (
                message(w.at[other, up_src, x, core], up_dst, up_dst, ups),
                message(w.at[other, down_src, x, core], down_dst, down_dst, downs),
            )
        up_dst, down_dst = w.at[other, 7, x, core, top], w.at[other, 7, x, core, bottom]
        return (
            message(w.at[other, 6, x, core, top], up_dst, up_dst, ups),
            message(w.at[other, 5, x, core, bottom], down_dst, down_dst, downs),
        )

    def xa(y_, group):
        slots = pl.ds(*groups[group])
        mine = w.at[y_, slots, x, core]
        return (
            message(mine, mine, w.at[y_, slots, x_left, core], rights),
            message(mine, mine, w.at[y_, slots, x_right, core], lefts),
        )

    def xa_far(y_, group):
        slots = pl.ds(*groups[group])
        from_left = w.at[y_, slots, x_left, core, top]
        from_right = w.at[y_, slots, x_right, core, bottom]
        return (
            message(from_left, from_left, w.at[y_, slots, x_far, core, top], rights),
            message(from_right, from_right, w.at[y_, slots, x_far, core, bottom], lefts),
        )

    def zb(step, x_, far_up):
        up_src, down_src = max(2 * step - 2, 0), max(2 * step - 3, 0)
        up_dst, down_dst = min(2 * step, 7), 2 * step - 1
        pair = ()
        if step < 4 or far_up:
            dst = w.at[own, up_dst, x_, core]
            pair += (message(w.at[own, up_src, x_, core], dst, dst, ups),)
        if step < 4 or not far_up:
            dst = w.at[own, down_dst, x_, core]
            pair += (message(w.at[own, down_src, x_, core], dst, dst, downs),)
        return pair

    za_m = {s: za(s) for s in (1, 2, 3, 4)}
    xa_m = {g: xa(other, g) for g in range(5)}
    xaf_m = {g: xa_far(other, g) for g in range(5)}
    xb_m, xbf_m = xa(own, 0), xa_far(own, 0)
    chains = {"mine": (x, True), "left": (x_left, True), "right": (x_right, False), "far": (x_far, False)}
    zb_m = {(c, s): zb(s, *chains[c]) for c in chains for s in (1, 2, 3, 4)}

    def zb_next(chain, step):
        recv_all(zb_m[chain, step])
        start_all(zb_m[chain, step + 1])

    def channel_at(lane, half_width):
        return (lane % half_width) // rows * (2 * rows) + lane // half_width * rows + lane % rows

    plain = (((1,), (0,)), ((), ()))
    group_count = rates.shape[1]
    lane = lax.broadcasted_iota(jnp.int32, (group_count, channels), 1)
    spread = (
        channel_at(lane, half) // (channels // group_count)
        == lax.broadcasted_iota(jnp.int32, (group_count, channels), 0)
    ).astype(jnp.float32)
    loads[0].wait()
    loads[1].wait()
    rate = lax.dot_general(rates[...], spread, plain, precision=HIGHEST, preferred_element_type=jnp.float32)
    residue = lax.dot_general(residues[...], spread, plain, precision=HIGHEST, preferred_element_type=jnp.float32)
    decay[...] = jnp.exp(-rate)
    coef[...] = residue * jnp.sqrt(2.0 * rate) * (1.0 / math.sqrt(poles))
    for k in range(LINE):
        rate_chunks[k] = rate[:, k * LANES : (k + 1) * LANES]

    loads[2].wait()
    pl.semaphore_wait(barrier, greetings)
    for way in range(3):
        tell(way, 0)
    start_all(xb_m)
    start_all(zb_m["mine", 1])

    rim_m = message(
        ext.at[:, pl.ds(tokens, RIM), :], ext.at[:, pl.ds(0, RIM), :], ext.at[:, pl.ds(0, RIM), :], (ctx + 1, tp)
    )
    eye = (
        lax.broadcasted_iota(jnp.int32, (tokens, tokens), 0)
        == lax.broadcasted_iota(jnp.int32, (tokens, tokens), 1)
    ).astype(jnp.bfloat16)
    loads[3].wait()
    for s in range(3):
        pairs = streams[s].reshape(channels // (2 * rows), 2, rows, tokens)
        for h in range(2):
            ext[s, pl.ds(RIM, tokens), pl.ds(h * half, half)] = lax.dot_general(
                eye, pairs[:, h].reshape(half, tokens), (((1,), (1,)), ((), ())), preferred_element_type=jnp.float32
            )
    pl.when(ctx < ctx_n - 1)(rim_m.start)
    pass_on(0)

    two = 2 * LANES
    order = (
        channel_at(lax.broadcasted_iota(jnp.int32, (two, two), 1), LANES)
        == lax.broadcasted_iota(jnp.int32, (two, two), 0)
    ).astype(jnp.float32)
    loads[4].wait()
    loads[5].wait()
    by_tap = jnp.concatenate([taps[s] for s in range(3)] + [skip[...]], axis=0)
    for k in range(channels // two):
        moved = lax.dot_general(
            by_tap[:, k * two : (k + 1) * two], order, plain, precision=HIGHEST, preferred_element_type=jnp.float32
        )
        for h in range(2):
            factors[:, pl.ds(h * half + k * LANES, LANES)] = moved[:, h * LANES : (h + 1) * LANES]

    def short_rows(first, length):
        def short(k, carry):
            lanes = pl.ds(pl.multiple_of(k * LANES, LANES), LANES)

            def filtered(s):
                total_ = None
                for shift in range(tap_count):
                    term = factors[pl.ds(s * tap_count + shift, 1), lanes] * ext[s, pl.ds(RIM + first - shift, length), lanes]
                    total_ = term if total_ is None else total_ + term
                return total_

            at_rows = pl.ds(first, length)
            query[at_rows, lanes] = filtered(0)
            gated[at_rows, lanes] = (filtered(1) * filtered(2)).astype(jnp.bfloat16).astype(jnp.float32)
            return carry

        lax.fori_loop(0, channels // LANES, short, 0)

    unroll = 8

    def run_states(first, length, lanes, state):
        fall = decay[:, lanes]

        def step(t, state):
            for u in range(unroll):
                state = state * fall + gated[pl.ds(first + t * unroll + u, 1), lanes]
            return state

        return lax.fori_loop(0, length // unroll, step, state)

    short_rows(RIM, tokens - RIM)
    pass_on(1)
    halves = [pl.ds(h * half, half) for h in range(2)]
    zeros = jnp.zeros((poles, half), jnp.float32)
    for h in range(2):
        state = run_states(RIM, tokens - RIM, halves[h], zeros)
        for k in range(half // LANES):
            ends[h * (half // LANES) + k] = state[:, k * LANES : (k + 1) * LANES]

    pass_on(2)
    start_all(across)

    @pl.when(ctx > 0)
    def _():
        rim_m.recv()

    @pl.when(ctx == 0)
    def _():
        for s in range(3):
            ext[s, pl.ds(0, RIM), :] = jnp.zeros((RIM, channels), jnp.float32)

    short_rows(0, RIM)
    for h in range(2):
        state = run_states(0, RIM, halves[h], zeros)
        for k in range(half // LANES):
            n = h * (half // LANES) + k
            ends[n] += state[:, k * LANES : (k + 1) * LANES] * jnp.exp(rate_chunks[n] * (-float(tokens - RIM)))

    round1 = []
    for m in range(1, LINE):
        to = flip(place, m)
        round1.append(message(ends.at[to], line_in.at[place], line_in.at[to], (ctx - place + to, tp)))
    start_all(round1)
    line_in[place] = ends[place]
    my_rate = rate_chunks[place]
    block_fall = jnp.exp(my_rate * (-float(tokens)))
    row_fall = jnp.exp(my_rate * (-float(tokens * LINE)))

    recv_all(xb_m)
    start_all(xbf_m)
    start_all(zb_m["right", 1])
    start_all(zb_m["left", 1])
    zb_next("mine", 1)
    pass_on(3)

    recv_all(round1)
    state = line_in[0]
    for p in range(1, LINE):
        state = state * block_fall + line_in[p]
    row_total[...] = state
    row_in[z] = state

    round2 = []
    for m in range(1, NZ):
        to = flip(z, m)
        round2.append(message(row_total, row_in.at[z], row_in.at[to], at(z_=to)))
    start_all(round2)

    recv_all(xbf_m)
    start_all(zb_m["far", 1])
    recv_all(across)
    start_all(za_m[1])
    start_all(xa_m[0])

    recv_all(round2)
    onward = []
    for m in range(LINE):
        far = flip(place, m)
        onward.append(
            message(part_total, part_in.at[place], part_in.at[far], ((ctx - place + far + ctx_n // 2) % ctx_n, tp))
        )

    @pl.when(y == 0)
    def _():
        state = row_in[0]
        for r in range(1, NZ):
            state = state * row_fall + row_in[r]
        part_total[...] = state
        for made in onward:
            made.start()

    state = jnp.zeros((poles, LANES), jnp.float32)
    for r in range(NZ - 1):
        state = jnp.where(r < z, state * row_fall + row_in[r], state)
    for p in range(LINE):
        enter_out[p] = state
        if p < LINE - 1:
            state = state * block_fall + line_in[p]

    round3 = []
    for m in range(1, LINE):
        to = flip(place, m)
        round3.append(message(enter_out.at[to], enter_in.at[place], enter_in.at[to], (ctx - place + to, tp)))
    start_all(round3)
    enter_in[place] = enter_out[place]

    zb_next("right", 1)
    zb_next("left", 1)
    recv_all(za_m[1])
    start_all(za_m[2])
    start_all(xa_m[1])
    recv_all(xa_m[0])
    start_all(xaf_m[0])
    zb_next("far", 1)
    zb_next("mine", 2)

    recv_all(round3)

    @pl.when(y == 1)
    def _():
        blocks = (ctx % (ctx_n // 2) * tokens).astype(jnp.float32)
        for n in range(LINE):
            since[n] = jnp.exp(rate_chunks[n] * -blocks)
        recv_all(onward)
        for n in range(LINE):
            enter_in[n] += since[n] * part_in[n]


    right_m, left_m = {}, {}
    up_tp, down_tp = (tp + 1) % tp_n, (tp + tp_n - 1) % tp_n
    home = message(outbox, mixed.at[core, tp], mixed.at[1 - core, tp], (sibling, tp))
    for r in range(2):
        of = core if r == 0 else 1 - core
        for d in range(3):
            behind, ahead = (tp + tp_n - d) % tp_n, (tp + d) % tp_n
            from_left, from_right = mixed.at[of, (tp + tp_n - 1 - d) % tp_n], mixed.at[of, (tp + 1 + d) % tp_n]
            if (r, d) == (1, 0):
                right_m[r, d] = message(outbox, mixed.at[core, tp], from_left, (sibling, up_tp))
                left_m[r, d] = message(outbox, mixed.at[core, tp], from_right, (sibling, down_tp))
            else:
                right_m[r, d] = message(mixed.at[of, behind], mixed.at[of, behind], from_left, (ctx, up_tp))
                left_m[r, d] = message(mixed.at[of, ahead], mixed.at[of, ahead], from_right, (ctx, down_tp))

    def line_send(r, d):
        pl.when((tp < tp_n - 1) & (tp >= d))(right_m[r, d].start)
        pl.when((tp > 0) & (tp + d < tp_n))(left_m[r, d].start)

    def line_sent(r, d):
        pl.when((tp < tp_n - 1) & (tp >= d))(right_m[r, d].sent)
        pl.when((tp > 0) & (tp + d < tp_n))(left_m[r, d].sent)

    def line_recv(r, d):
        pl.when(tp >= d + 1)(right_m[r, d].recv)
        pl.when(tp + d + 1 < tp_n)(left_m[r, d].recv)

    for r in (1, 0):
        which = core if r == 0 else 1 - core
        lanes = pl.ds(pl.multiple_of(which * half, half), half)
        fall, gain = decay[:, lanes], coef[:, lanes]
        first = which * (half // LANES)
        enter = jnp.concatenate([enter_in[first + k] for k in range(half // LANES)], axis=1)

        def step(t, state):
            for u in range(unroll):
                at_t = pl.ds(t * unroll + u, 1)
                state = state * fall + gated[at_t, lanes]
                conv[at_t, :] = jnp.sum(state * gain, axis=0, keepdims=True)
            return state

        lax.fori_loop(0, tokens // unroll, step, enter)
        block = (
            query[:, lanes] * (conv[...] + factors[pl.ds(3 * tap_count, 1), lanes] * gated[:, lanes])
        ).astype(jnp.bfloat16)
        if r == 1:
            outbox[...] = block
            start_all((home,))
        else:
            mixed[core, tp] = block
        line_send(r, 0)
        if r == 1:
            recv_all(za_m[2])
            start_all(za_m[3])
            start_all(xa_m[2])
            zb_next("right", 2)
            zb_next("left", 2)
            recv_all(xa_m[1])
            start_all(xaf_m[1])

    recv_all(za_m[3])
    start_all(za_m[4])
    start_all(xa_m[3])
    zb_next("far", 2)
    recv_all(xa_m[2])
    start_all(xaf_m[2])
    zb_next("mine", 3)
    line_recv(1, 0)
    line_send(1, 1)
    zb_next("right", 3)
    recv_all(za_m[4])
    start_all(xa_m[4])
    zb_next("left", 3)
    zb_next("far", 3)
    line_recv(0, 0)
    line_send(0, 1)
    recv_all(xa_m[3])
    start_all(xaf_m[3])
    recv_all(xa_m[4])
    start_all(xaf_m[4])
    line_recv(1, 1)
    line_send(1, 2)
    recv_all((home,))

    deep = NX * rows
    total[...] = jnp.zeros_like(total)

    def slot_of(z_):
        behind = (z_ + NZ - z) % NZ
        return jnp.where(behind <= 4, jnp.maximum(2 * behind - 1, 0), 2 * (NZ - behind))

    def tokens_of(c):
        return pl.ds(pl.multiple_of(c * tokens, tokens), tokens)

    last_pair = ((z + NZ // 2) % NZ) // 2

    def project(distances, late, only=None):
        def step(n, carry):
            y_, pair = n // 4, n % 4
            block = y_ * 2 + pair // 2
            distance = jnp.maximum(block - tp, tp - block)
            wanted = (distance >= distances[0]) & (distance <= distances[1])
            if late is not None:
                wanted = wanted & ((pair == last_pair) if late else (pair != last_pair))

            @pl.when(wanted)
            def _():
                weights = jnp.concatenate(
                    [
                        w[y_, slot_of(2 * pair + k), pl.ds(0, NX), core].reshape(deep, w.shape[-1])
                        for k in range(2)
                    ],
                    axis=0,
                )
                part = pl.ds(pl.multiple_of((pair % 2) * 2 * deep, 2 * deep), 2 * deep)
                if only is None:
                    left = jnp.concatenate([mixed[c, block, :, part] for c in range(2)], axis=0)
                    total[...] += jnp.dot(left, weights, preferred_element_type=jnp.float32)
                else:
                    total[tokens_of(only), :] += jnp.dot(
                        mixed[only, block, :, part], weights, preferred_element_type=jnp.float32
                    )

            return carry

        lax.fori_loop(0, 2 * NZ // 2, step, 0)

    for g in range(4):
        recv_all(xaf_m[g])
    project((0, 0), False)
    line_recv(0, 1)
    line_send(0, 2)
    project((1, 2), False)
    recv_all(xaf_m[4])
    for c in chains:
        recv_all(zb_m[c, 4])
    project((0, 2), True)
    line_recv(1, 2)
    project((3, 3), None, 1 - core)
    part_out[...] = total[tokens_of(1 - core), :].astype(jnp.bfloat16)
    swap = message(part_out, part_back, part_back, (sibling, tp))
    start_all((swap,))
    line_recv(0, 2)
    project((3, 3), None, core)
    recv_all((swap,))
    out[...] = (total[tokens_of(core), :] + part_back[...].astype(jnp.float32)).astype(jnp.bfloat16)

    for made in sent:
        made.sent()
    pl.when(ctx < ctx_n - 1)(rim_m.sent)

    @pl.when(y == 0)
    def _():
        for made in onward:
            made.sent()

    for r in range(2):
        for d in range(3):
            line_sent(r, d)


def local(streams, conv_weight, rates, residues, skip, out_weight):
    channels, tokens = streams.shape[1:]
    groups, poles = rates.shape
    rows, features = out_weight.shape
    anywhere = pl.BlockSpec(memory_space=pl.ANY)
    f32, bf16 = jnp.float32, jnp.bfloat16
    messages = 1 + 8 + 20 + 4 + 28 + 1 + 7 + 7 + 8 + 7 + 13 + 1
    return pl.pallas_call(
        functools.partial(kernel, conv_weight.shape[1]),
        out_shape=jax.ShapeDtypeStruct((tokens, features), bf16),
        in_specs=[anywhere] * 6,
        out_specs=pl.BlockSpec(memory_space=pltpu.VMEM),
        scratch_shapes=[
            pltpu.VMEM((2, NZ, NX, 2, rows, features), bf16),
            pltpu.VMEM(streams.shape, bf16),
            pltpu.VMEM(conv_weight.shape, f32),
            pltpu.VMEM((poles, groups), f32),
            pltpu.VMEM((poles, groups), f32),
            pltpu.VMEM((1, channels), f32),
            pltpu.VMEM((3, RIM + tokens, channels), f32),
            pltpu.VMEM((tokens, channels), f32),
            pltpu.VMEM((tokens, channels), f32),
            pltpu.VMEM((tokens, channels // 2), f32),
            pltpu.VMEM((3 * conv_weight.shape[1] + 1, channels), f32),
            pltpu.VMEM((poles, channels), f32),
            pltpu.VMEM((poles, channels), f32),
            pltpu.VMEM((LINE, poles, LANES), f32),
            pltpu.VMEM((LINE, poles, LANES), f32),
            pltpu.VMEM((LINE, poles, LANES), f32),
            pltpu.VMEM((poles, LANES), f32),
            pltpu.VMEM((NZ, poles, LANES), f32),
            pltpu.VMEM((poles, LANES), f32),
            pltpu.VMEM((LINE, poles, LANES), f32),
            pltpu.VMEM((LINE, poles, LANES), f32),
            pltpu.VMEM((LINE, poles, LANES), f32),
            pltpu.VMEM((LINE, poles, LANES), f32),
            pltpu.VMEM((2, 4, tokens, channels // 2), bf16),
            pltpu.VMEM((tokens, channels // 2), bf16),
            pltpu.VMEM((tokens, features), bf16),
            pltpu.VMEM((tokens, features), bf16),
            pltpu.VMEM((2 * tokens, features), f32),
            pltpu.SemaphoreType.REGULAR((3, 4)),
            pltpu.SemaphoreType.DMA((6,)),
            pltpu.SemaphoreType.DMA((messages,)),
            pltpu.SemaphoreType.DMA((messages,)),
        ],
        compiler_params=pltpu.CompilerParams(
            collective_id=0, has_side_effects=True, vmem_limit_bytes=60 * 1024 * 1024
        ),
        cost_estimate=pl.CostEstimate(
            flops=2 * tokens * 4 * channels * features, bytes_accessed=12 << 20, transcendentals=1 << 15
        ),
    )(streams, conv_weight, rates.T, residues.T, skip.reshape(1, channels), out_weight)


def solution(mesh):
    return jax.shard_map(
        local,
        mesh=mesh,
        in_specs=(
            P(None, "tp", "ctx"),
            P(None, None, "tp"),
            P("tp", None),
            P("tp", None),
            P("tp"),
            P("ctx", "tp"),
        ),
        out_specs=P("ctx", "tp"),
        check_vma=False,
    )
```

```python
import functools
import math

import jax
import jax.numpy as jnp
from jax import lax
from jax.experimental import pallas as pl
from jax.experimental.pallas import tpu as pltpu
from jax.sharding import PartitionSpec as P

NZ, NX = 8, 4
LINE = NX * 2
LANES = 128
RIM = 8
HIGHEST = lax.Precision.HIGHEST


class Message:
    def __init__(self, sems, number, src, dst, land, to):
        send, recv = sems
        make = functools.partial(
            pltpu.make_async_remote_copy,
            send_sem=send.at[number],
            recv_sem=recv.at[number],
            device_id=to,
            device_id_type=pl.DeviceIdType.MESH,
        )
        self.out = make(src_ref=src, dst_ref=dst)
        self.into = make(src_ref=src, dst_ref=land)

    def start(self):
        self.out.start()

    def recv(self):
        self.into.wait_recv()

    def sent(self):
        self.out.wait_send()


def kernel(
    tap_count,
    streams_hbm,
    taps_hbm,
    rates_hbm,
    residues_hbm,
    skip_hbm,
    w_hbm,
    out,
    w,
    streams,
    taps,
    rates,
    residues,
    skip,
    ext,
    query,
    gated,
    conv,
    factors,
    decay,
    coef,
    rate_chunks,
    ends,
    line_in,
    row_total,
    row_in,
    part_total,
    part_in,
    since,
    enter_out,
    enter_in,
    mixed,
    outbox,
    part_out,
    part_back,
    total,
    heard,
    load_sems,
    send_sems,
    recv_sems,
):
    poles = rates.shape[0]
    channels, tokens = streams.shape[1:]
    half = channels // 2
    rows = w_hbm.shape[0]
    ctx, tp = lax.axis_index("ctx"), lax.axis_index("tp")
    ctx_n, tp_n = lax.axis_size("ctx"), lax.axis_size("tp")
    core = ctx % 2
    x = (ctx // 2) % NX
    z = (ctx // LINE) % NZ
    y = ctx // (LINE * NZ)
    place = ctx % LINE

    def at(y_=None, z_=None, x_=None, core_=None):
        y_ = y if y_ is None else y_
        z_ = z if z_ is None else z_
        x_ = x if x_ is None else x_
        core_ = core if core_ is None else core_
        return (((y_ * NZ + z_) * NX + x_) * 2 + core_, tp)

    def flip(value, bits):
        result = value * 0
        for bit in (1, 2, 4):
            digit = (value // bit) % 2
            result = result + bit * ((1 - digit) if bits & bit else digit)
        return result

    sems = (send_sems, recv_sems)
    count = [0]
    sent = []

    def message(src, dst, land, to):
        made = Message(sems, count[0], src, dst, land, to)
        count[0] += 1
        return made

    def start_all(pair):
        for made in pair:
            made.start()
            sent.append(made)

    def recv_all(pair):
        for made in pair:
            made.recv()

    barrier = pltpu.get_barrier_semaphore()

    def greet(peer):
        pl.semaphore_signal(barrier, inc=1, device_id=peer, device_id_type=pl.DeviceIdType.MESH)

    sibling = at(core_=1 - core)[0]
    ups, downs = at(z_=(z + 1) % NZ), at(z_=(z + NZ - 1) % NZ)
    wraps_up, wraps_down = tp == tp_n - 1, tp == 0
    crossed = (ctx + ctx_n // 2) % ctx_n
    onwards = (jnp.where(wraps_up, crossed, ctx), jnp.where(wraps_up, 0, tp + 1))
    backwards = (jnp.where(wraps_down, crossed, ctx), jnp.where(wraps_down, tp_n - 1, tp - 1))
    always = [ups, downs, onwards, backwards]
    always += [(ctx - place + flip(place, m), tp) for m in range(LINE - 1, 0, -1)]
    for peer in always:
        greet(peer)
    pl.when(ctx > 0)(functools.partial(greet, (ctx - 1, tp)))
    pl.when(tp < tp_n - 1)(functools.partial(greet, (sibling, tp + 1)))
    pl.when(tp > 0)(functools.partial(greet, (sibling, tp - 1)))
    greetings = len(always)
    for there in (ctx < ctx_n - 1, tp < tp_n - 1, tp > 0):
        greetings = greetings + there.astype(jnp.int32)

    ways = [ups, downs, onwards]
    last_step = [2, 2, 3]

    def tell(way, step):
        pl.semaphore_signal(
            heard.at[way, step], inc=1, device_id=ways[way], device_id_type=pl.DeviceIdType.MESH
        )

    def pass_on(step):
        for way in range(3):
            if step <= last_step[way]:
                pl.semaphore_wait(heard.at[way, step], 1)
            if step < last_step[way]:
                tell(way, step + 1)

    loads = [
        pltpu.make_async_copy(src, dst, load_sems.at[n])
        for n, (src, dst) in enumerate(
            [
                (rates_hbm, rates),
                (residues_hbm, residues),
                (w_hbm, w.at[y, 0, x, core]),
                (streams_hbm, streams),
                (taps_hbm, taps),
                (skip_hbm, skip),
            ]
        )
    ]
    for load in loads:
        load.start()

    groups = [(0, 1), (1, 2), (3, 2), (5, 2), (7, 1)]
    rights, lefts = at(x_=(x + 1) % NX), at(x_=(x + NX - 1) % NX)
    x_left, x_right = (x + NX - 1) % NX, (x + 1) % NX
    x_far = (x + 2) % NX
    top, bottom = pl.ds(0, rows // 2), pl.ds(rows // 2, rows // 2)
    own, other = y, 1 - y

    across = (message(w.at[own, 0, x, core], w.at[own, 0, x, core], w.at[other, 0, x, core], at(y_=other)),)

    def za(step):
        up_src, down_src = max(2 * step - 2, 0), max(2 * step - 3, 0)
        if step < 4:
            up_dst, down_dst = w.at[other, 2 * step, x, core], w.at[other, 2 * step - 1, x, core]
            return (
                message(w.at[other, up_src, x, core], up_dst, up_dst, ups),
                message(w.at[other, down_src, x, core], down_dst, down_dst, downs),
            )
        up_dst, down_dst = w.at[other, 7, x, core, top], w.at[other, 7, x, core, bottom]
        return (
            message(w.at[other, 6, x, core, top], up_dst, up_dst, ups),
            message(w.at[other, 5, x, core, bottom], down_dst, down_dst, downs),
        )

    def xa(y_, group):
        slots = pl.ds(*groups[group])
        mine = w.at[y_, slots, x, core]
        return (
            message(mine, mine, w.at[y_, slots, x_left, core], rights),
            message(mine, mine, w.at[y_, slots, x_right, core], lefts),
        )

    def xa_far(y_, group):
        slots = pl.ds(*groups[group])
        from_left = w.at[y_, slots, x_left, core, top]
        from_right = w.at[y_, slots, x_right, core, bottom]
        return (
            message(from_left, from_left, w.at[y_, slots, x_far, core, top], rights),
            message(from_right, from_right, w.at[y_, slots, x_far, core, bottom], lefts),
        )

    def zb(step, x_, far_up):
        up_src, down_src = max(2 * step - 2, 0), max(2 * step - 3, 0)
        up_dst, down_dst = min(2 * step, 7), 2 * step - 1
        pair = ()
        if step < 4 or far_up:
            dst = w.at[own, up_dst, x_, core]
            pair += (message(w.at[own, up_src, x_, core], dst, dst, ups),)
        if step < 4 or not far_up:
            dst = w.at[own, down_dst, x_, core]
            pair += (message(w.at[own, down_src, x_, core], dst, dst, downs),)
        return pair

    za_m = {s: za(s) for s in (1, 2, 3, 4)}
    xa_m = {g: xa(other, g) for g in range(5)}
    xaf_m = {g: xa_far(other, g) for g in range(5)}
    xb_m, xbf_m = xa(own, 0), xa_far(own, 0)
    chains = {"mine": (x, True), "left": (x_left, True), "right": (x_right, False), "far": (x_far, False)}
    zb_m = {(c, s): zb(s, *chains[c]) for c in chains for s in (1, 2, 3, 4)}

    def zb_next(chain, step):
        recv_all(zb_m[chain, step])
        start_all(zb_m[chain, step + 1])

    def channel_at(lane, half_width):
        return (lane % half_width) // rows * (2 * rows) + lane // half_width * rows + lane % rows

    plain = (((1,), (0,)), ((), ()))
    group_count = rates.shape[1]
    lane = lax.broadcasted_iota(jnp.int32, (group_count, channels), 1)
    spread = (
        channel_at(lane, half) // (channels // group_count)
        == lax.broadcasted_iota(jnp.int32, (group_count, channels), 0)
    ).astype(jnp.float32)
    loads[0].wait()
    loads[1].wait()
    rate = lax.dot_general(rates[...], spread, plain, precision=HIGHEST, preferred_element_type=jnp.float32)
    residue = lax.dot_general(residues[...], spread, plain, precision=HIGHEST, preferred_element_type=jnp.float32)
    decay[...] = jnp.exp(-rate)
    coef[...] = residue * jnp.sqrt(2.0 * rate) * (1.0 / math.sqrt(poles))
    for k in range(LINE):
        rate_chunks[k] = rate[:, k * LANES : (k + 1) * LANES]

    loads[2].wait()
    pl.semaphore_wait(barrier, greetings)
    for way in range(3):
        tell(way, 0)
    start_all(xb_m)
    start_all(zb_m["mine", 1])

    rim_m = message(
        ext.at[:, pl.ds(tokens, RIM), :], ext.at[:, pl.ds(0, RIM), :], ext.at[:, pl.ds(0, RIM), :], (ctx + 1, tp)
    )
    eye = (
        lax.broadcasted_iota(jnp.int32, (tokens, tokens), 0)
        == lax.broadcasted_iota(jnp.int32, (tokens, tokens), 1)
    ).astype(jnp.bfloat16)
    loads[3].wait()
    for s in range(3):
        pairs = streams[s].reshape(channels // (2 * rows), 2, rows, tokens)
        for h in range(2):
            ext[s, pl.ds(RIM, tokens), pl.ds(h * half, half)] = lax.dot_general(
                eye, pairs[:, h].reshape(half, tokens), (((1,), (1,)), ((), ())), preferred_element_type=jnp.float32
            )
    pl.when(ctx < ctx_n - 1)(rim_m.start)

    two = 2 * LANES
    order = (
        channel_at(lax.broadcasted_iota(jnp.int32, (two, two), 1), LANES)
        == lax.broadcasted_iota(jnp.int32, (two, two), 0)
    ).astype(jnp.float32)
    loads[4].wait()
    loads[5].wait()
    by_tap = jnp.concatenate([taps[s] for s in range(3)] + [skip[...]], axis=0)
    for k in range(channels // two):
        moved = lax.dot_general(
            by_tap[:, k * two : (k + 1) * two], order, plain, precision=HIGHEST, preferred_element_type=jnp.float32
        )
        for h in range(2):
            factors[:, pl.ds(h * half + k * LANES, LANES)] = moved[:, h * LANES : (h + 1) * LANES]

    def short_rows(first, length):
        def short(k, carry):
            lanes = pl.ds(pl.multiple_of(k * LANES, LANES), LANES)

            def filtered(s):
                total_ = None
                for shift in range(tap_count):
                    term = factors[pl.ds(s * tap_count + shift, 1), lanes] * ext[s, pl.ds(RIM + first - shift, length), lanes]
                    total_ = term if total_ is None else total_ + term
                return total_

            at_rows = pl.ds(first, length)
            query[at_rows, lanes] = filtered(0)
            gated[at_rows, lanes] = (filtered(1) * filtered(2)).astype(jnp.bfloat16).astype(jnp.float32)
            return carry

        lax.fori_loop(0, channels // LANES, short, 0)

    unroll = 8

    def run_states(first, length, lanes, state):
        fall = decay[:, lanes]

        def step(t, state):
            for u in range(unroll):
                state = state * fall + gated[pl.ds(first + t * unroll + u, 1), lanes]
            return state

        return lax.fori_loop(0, length // unroll, step, state)

    pass_on(0)
    short_rows(RIM, tokens - RIM)
    pass_on(1)
    halves = [pl.ds(h * half, half) for h in range(2)]
    zeros = jnp.zeros((poles, half), jnp.float32)
    for h in range(2):
        state = run_states(RIM, tokens - RIM, halves[h], zeros)
        for k in range(half // LANES):
            ends[h * (half // LANES) + k] = state[:, k * LANES : (k + 1) * LANES]

    pass_on(2)
    start_all(across)

    @pl.when(ctx > 0)
    def _():
        rim_m.recv()

    @pl.when(ctx == 0)
    def _():
        for s in range(3):
            ext[s, pl.ds(0, RIM), :] = jnp.zeros((RIM, channels), jnp.float32)

    short_rows(0, RIM)
    for h in range(2):
        state = run_states(0, RIM, halves[h], zeros)
        for k in range(half // LANES):
            n = h * (half // LANES) + k
            ends[n] += state[:, k * LANES : (k + 1) * LANES] * jnp.exp(rate_chunks[n] * (-float(tokens - RIM)))

    round1 = []
    for m in range(1, LINE):
        to = flip(place, m)
        round1.append(message(ends.at[to], line_in.at[place], line_in.at[to], (ctx - place + to, tp)))
    start_all(round1)
    line_in[place] = ends[place]
    my_rate = rate_chunks[place]
    block_fall = jnp.exp(my_rate * (-float(tokens)))
    row_fall = jnp.exp(my_rate * (-float(tokens * LINE)))

    recv_all(xb_m)
    start_all(xbf_m)
    start_all(zb_m["right", 1])
    start_all(zb_m["left", 1])
    zb_next("mine", 1)
    pass_on(3)

    recv_all(round1)
    state = line_in[0]
    for p in range(1, LINE):
        state = state * block_fall + line_in[p]
    row_total[...] = state
    row_in[z] = state

    round2 = []
    for m in range(1, NZ):
        to = flip(z, m)
        round2.append(message(row_total, row_in.at[z], row_in.at[to], at(z_=to)))
    start_all(round2)

    recv_all(xbf_m)
    start_all(zb_m["far", 1])
    recv_all(across)
    start_all(za_m[1])
    start_all(xa_m[0])

    recv_all(round2)
    onward = []
    for m in range(LINE):
        far = flip(place, m)
        onward.append(
            message(part_total, part_in.at[place], part_in.at[far], ((ctx - place + far + ctx_n // 2) % ctx_n, tp))
        )

    @pl.when(y == 0)
    def _():
        state = row_in[0]
        for r in range(1, NZ):
            state = state * row_fall + row_in[r]
        part_total[...] = state
        for made in onward:
            made.start()

    state = jnp.zeros((poles, LANES), jnp.float32)
    for r in range(NZ - 1):
        state = jnp.where(r < z, state * row_fall + row_in[r], state)
    for p in range(LINE):
        enter_out[p] = state
        if p < LINE - 1:
            state = state * block_fall + line_in[p]

    round3 = []
    for m in range(1, LINE):
        to = flip(place, m)
        round3.append(message(enter_out.at[to], enter_in.at[place], enter_in.at[to], (ctx - place + to, tp)))
    start_all(round3)
    enter_in[place] = enter_out[place]

    zb_next("right", 1)
    zb_next("left", 1)
    recv_all(za_m[1])
    start_all(za_m[2])
    start_all(xa_m[1])
    recv_all(xa_m[0])
    start_all(xaf_m[0])
    zb_next("far", 1)
    zb_next("mine", 2)

    recv_all(round3)

    @pl.when(y == 1)
    def _():
        blocks = (ctx % (ctx_n // 2) * tokens).astype(jnp.float32)
        for n in range(LINE):
            since[n] = jnp.exp(rate_chunks[n] * -blocks)
        recv_all(onward)
        for n in range(LINE):
            enter_in[n] += since[n] * part_in[n]


    right_m, left_m = {}, {}
    up_tp, down_tp = (tp + 1) % tp_n, (tp + tp_n - 1) % tp_n
    home = message(outbox, mixed.at[core, tp], mixed.at[1 - core, tp], (sibling, tp))
    for r in range(2):
        of = core if r == 0 else 1 - core
        for d in range(3):
            behind, ahead = (tp + tp_n - d) % tp_n, (tp + d) % tp_n
            from_left, from_right = mixed.at[of, (tp + tp_n - 1 - d) % tp_n], mixed.at[of, (tp + 1 + d) % tp_n]
            if (r, d) == (1, 0):
                right_m[r, d] = message(outbox, mixed.at[core, tp], from_left, (sibling, up_tp))
                left_m[r, d] = message(outbox, mixed.at[core, tp], from_right, (sibling, down_tp))
            else:
                right_m[r, d] = message(mixed.at[of, behind], mixed.at[of, behind], from_left, (ctx, up_tp))
                left_m[r, d] = message(mixed.at[of, ahead], mixed.at[of, ahead], from_right, (ctx, down_tp))

    def line_send(r, d):
        pl.when((tp < tp_n - 1) & (tp >= d))(right_m[r, d].start)
        pl.when((tp > 0) & (tp + d < tp_n))(left_m[r, d].start)

    def line_sent(r, d):
        pl.when((tp < tp_n - 1) & (tp >= d))(right_m[r, d].sent)
        pl.when((tp > 0) & (tp + d < tp_n))(left_m[r, d].sent)

    def line_recv(r, d):
        pl.when(tp >= d + 1)(right_m[r, d].recv)
        pl.when(tp + d + 1 < tp_n)(left_m[r, d].recv)

    for r in (1, 0):
        which = core if r == 0 else 1 - core
        lanes = pl.ds(pl.multiple_of(which * half, half), half)
        fall, gain = decay[:, lanes], coef[:, lanes]
        first = which * (half // LANES)
        enter = jnp.concatenate([enter_in[first + k] for k in range(half // LANES)], axis=1)

        def step(t, state):
            for u in range(unroll):
                at_t = pl.ds(t * unroll + u, 1)
                state = state * fall + gated[at_t, lanes]
                conv[at_t, :] = jnp.sum(state * gain, axis=0, keepdims=True)
            return state

        lax.fori_loop(0, tokens // unroll, step, enter)
        block = (
            query[:, lanes] * (conv[...] + factors[pl.ds(3 * tap_count, 1), lanes] * gated[:, lanes])
        ).astype(jnp.bfloat16)
        if r == 1:
            outbox[...] = block
            start_all((home,))
        else:
            mixed[core, tp] = block
        line_send(r, 0)
        if r == 1:
            recv_all(za_m[2])
            start_all(za_m[3])
            start_all(xa_m[2])
            zb_next("right", 2)
            zb_next("left", 2)
            recv_all(xa_m[1])
            start_all(xaf_m[1])

    recv_all(za_m[3])
    start_all(za_m[4])
    start_all(xa_m[3])
    zb_next("far", 2)
    recv_all(xa_m[2])
    start_all(xaf_m[2])
    zb_next("mine", 3)
    line_recv(1, 0)
    line_send(1, 1)
    zb_next("right", 3)
    recv_all(za_m[4])
    start_all(xa_m[4])
    zb_next("left", 3)
    zb_next("far", 3)
    line_recv(0, 0)
    line_send(0, 1)
    recv_all(xa_m[3])
    start_all(xaf_m[3])
    recv_all(xa_m[4])
    start_all(xaf_m[4])
    line_recv(1, 1)
    line_send(1, 2)
    recv_all((home,))

    deep = NX * rows
    total[...] = jnp.zeros_like(total)

    def slot_of(z_):
        behind = (z_ + NZ - z) % NZ
        return jnp.where(behind <= 4, jnp.maximum(2 * behind - 1, 0), 2 * (NZ - behind))

    def tokens_of(c):
        return pl.ds(pl.multiple_of(c * tokens, tokens), tokens)

    last_pair = ((z + NZ // 2) % NZ) // 2

    def project(distances, late, only=None):
        def step(n, carry):
            y_, pair = n // 4, n % 4
            block = y_ * 2 + pair // 2
            distance = jnp.maximum(block - tp, tp - block)
            wanted = (distance >= distances[0]) & (distance <= distances[1])
            if late is not None:
                wanted = wanted & ((pair == last_pair) if late else (pair != last_pair))

            @pl.when(wanted)
            def _():
                weights = jnp.concatenate(
                    [
                        w[y_, slot_of(2 * pair + k), pl.ds(0, NX), core].reshape(deep, w.shape[-1])
                        for k in range(2)
                    ],
                    axis=0,
                )
                part = pl.ds(pl.multiple_of((pair % 2) * 2 * deep, 2 * deep), 2 * deep)
                if only is None:
                    left = jnp.concatenate([mixed[c, block, :, part] for c in range(2)], axis=0)
                    total[...] += jnp.dot(left, weights, preferred_element_type=jnp.float32)
                else:
                    total[tokens_of(only), :] += jnp.dot(
                        mixed[only, block, :, part], weights, preferred_element_type=jnp.float32
                    )

            return carry

        lax.fori_loop(0, 2 * NZ // 2, step, 0)

    for g in range(4):
        recv_all(xaf_m[g])
    project((0, 0), False)
    line_recv(0, 1)
    line_send(0, 2)
    project((1, 2), False)
    recv_all(xaf_m[4])
    for c in chains:
        recv_all(zb_m[c, 4])
    project((0, 2), True)
    line_recv(1, 2)
    project((3, 3), None, 1 - core)
    part_out[...] = total[tokens_of(1 - core), :].astype(jnp.bfloat16)
    swap = message(part_out, part_back, part_back, (sibling, tp))
    start_all((swap,))
    line_recv(0, 2)
    project((3, 3), None, core)
    recv_all((swap,))
    out[...] = (total[tokens_of(core), :] + part_back[...].astype(jnp.float32)).astype(jnp.bfloat16)

    for made in sent:
        made.sent()
    pl.when(ctx < ctx_n - 1)(rim_m.sent)

    @pl.when(y == 0)
    def _():
        for made in onward:
            made.sent()

    for r in range(2):
        for d in range(3):
            line_sent(r, d)


def local(streams, conv_weight, rates, residues, skip, out_weight):
    channels, tokens = streams.shape[1:]
    groups, poles = rates.shape
    rows, features = out_weight.shape
    anywhere = pl.BlockSpec(memory_space=pl.ANY)
    f32, bf16 = jnp.float32, jnp.bfloat16
    messages = 1 + 8 + 20 + 4 + 28 + 1 + 7 + 7 + 8 + 7 + 13 + 1
    return pl.pallas_call(
        functools.partial(kernel, conv_weight.shape[1]),
        out_shape=jax.ShapeDtypeStruct((tokens, features), bf16),
        in_specs=[anywhere] * 6,
        out_specs=pl.BlockSpec(memory_space=pltpu.VMEM),
        scratch_shapes=[
            pltpu.VMEM((2, NZ, NX, 2, rows, features), bf16),
            pltpu.VMEM(streams.shape, bf16),
            pltpu.VMEM(conv_weight.shape, f32),
            pltpu.VMEM((poles, groups), f32),
            pltpu.VMEM((poles, groups), f32),
            pltpu.VMEM((1, channels), f32),
            pltpu.VMEM((3, RIM + tokens, channels), f32),
            pltpu.VMEM((tokens, channels), f32),
            pltpu.VMEM((tokens, channels), f32),
            pltpu.VMEM((tokens, channels // 2), f32),
            pltpu.VMEM((3 * conv_weight.shape[1] + 1, channels), f32),
            pltpu.VMEM((poles, channels), f32),
            pltpu.VMEM((poles, channels), f32),
            pltpu.VMEM((LINE, poles, LANES), f32),
            pltpu.VMEM((LINE, poles, LANES), f32),
            pltpu.VMEM((LINE, poles, LANES), f32),
            pltpu.VMEM((poles, LANES), f32),
            pltpu.VMEM((NZ, poles, LANES), f32),
            pltpu.VMEM((poles, LANES), f32),
            pltpu.VMEM((LINE, poles, LANES), f32),
            pltpu.VMEM((LINE, poles, LANES), f32),
            pltpu.VMEM((LINE, poles, LANES), f32),
            pltpu.VMEM((LINE, poles, LANES), f32),
            pltpu.VMEM((2, 4, tokens, channels // 2), bf16),
            pltpu.VMEM((tokens, channels // 2), bf16),
            pltpu.VMEM((tokens, features), bf16),
            pltpu.VMEM((tokens, features), bf16),
            pltpu.VMEM((2 * tokens, features), f32),
            pltpu.SemaphoreType.REGULAR((3, 4)),
            pltpu.SemaphoreType.DMA((6,)),
            pltpu.SemaphoreType.DMA((messages,)),
            pltpu.SemaphoreType.DMA((messages,)),
        ],
        compiler_params=pltpu.CompilerParams(
            collective_id=0, has_side_effects=True, vmem_limit_bytes=60 * 1024 * 1024
        ),
        cost_estimate=pl.CostEstimate(
            flops=2 * tokens * 4 * channels * features, bytes_accessed=12 << 20, transcendentals=1 << 15
        ),
    )(streams, conv_weight, rates.T, residues.T, skip.reshape(1, channels), out_weight)


def solution(mesh):
    return jax.shard_map(
        local,
        mesh=mesh,
        in_specs=(
            P(None, "tp", "ctx"),
            P(None, None, "tp"),
            P("tp", None),
            P("tp", None),
            P("tp"),
            P("ctx", "tp"),
        ),
        out_specs=P("ctx", "tp"),
        check_vma=False,
    )
```
